32 devices in a mesh: sect: 4 (over y, x), dp: 4 (over z), tp: 2 (over core).
Axes of the slice: x: 2, y: 2, z: 4, core: 2. Of those that a mesh axis runs over, the one named last changes fastest.
Arguments:
- queries: bfloat16 [4, 64, 48, 128], P('dp', 'sect', 'tp'), may hold values from -250 to 250
- key_cache: bfloat16 [4, 64, 8, 192, 128], P('dp', 'sect', 'tp'), may hold values from -6 to 6
- cached_values: bfloat16 [4, 64, 8, 192, 128], P('dp', 'sect', 'tp'), may hold values from -12 to 12
- incoming_keys: bfloat16 [4, 64, 8, 128], P('dp', 'sect', 'tp'), may hold values from -12 to 12
- incoming_values: bfloat16 [4, 64, 8, 128], P('dp', 'sect', 'tp'), may hold values from -12 to 12
- lengths: int32 [4, 64], P('dp', 'sect'), may hold values from 2 to 192, as said below
- residual: bfloat16 [256, 6144], P('dp', ('sect', 'tp')), may hold values from -8 to 8
- out_proj: bfloat16 [6144, 6144], P(None, ('sect', 'tp')), may hold values from -0.078125 to 0.078125
- norm_gain: float32 [6144], replicated, may hold values from 0.1 to 1.9
- router: bfloat16 [6144, 4], replicated, may hold values from -0.21875 to 0.21875
- gate_proj: bfloat16 [4, 6144, 8192], P('dp', 'sect', 'tp'), may hold values from -0.078125 to 0.078125
- up_proj: bfloat16 [4, 6144, 8192], P('dp', 'sect', 'tp'), may hold values from -0.078125 to 0.078125
- down_proj: bfloat16 [4, 8192, 6144], P('dp', 'tp', 'sect'), may hold values from -0.09375 to 0.09375
- routes: int32 [256, 2], P('dp'), may hold values from 0 to 3, as said below
Outputs:
- mixed: bfloat16 [256, 6144], P('dp', ('sect', 'tp'))
The draws below stay inside these ranges and needn't reach their ends.
Inputs may be any that keep to these rules, and one draw needn't show every extreme that they name: `lengths`: each sequence has 2 or more filled slots; some sequence has all 192 filled. `routes`: the two experts of a token differ. In each block of 64 tokens held by one index of dp, no expert is named by more than 32 tokens, and the same expert is named by exactly 32 tokens in every block.
All inputs are finite; a program needn't handle non-finite values.
Results may differ from the reference program's by a relative error of at most 0.022.
Values may be sent and summed in bfloat16 or wider, within the bound.
A program may use at most 128 MiB of HBM per device.

```python
import math
import jax
import jax.numpy as jnp
from jax import lax

D = 6144
QUERY_HEADS = 48
KEY_VALUE_HEADS = 8
HEAD_DIM = 128
FFW = 8192
CONTEXT_SLOTS = 192
EXPERTS = 4
GROUP_TOKENS = 64
BATCH = 256
CAP = 32
N_DP = 4


def loguniform_draw(key, shape, lowest, highest):
    return jnp.exp(jax.random.uniform(key, shape, jnp.float32, jnp.log(lowest), jnp.log(highest)))


def attention_pair(key):
    queries = jnp.clip(jax.random.normal(jax.random.fold_in(key, 12), (N_DP, GROUP_TOKENS, QUERY_HEADS, HEAD_DIM), jnp.float32), -6.0, 6.0)
    cached_entries = jnp.clip(jax.random.normal(jax.random.fold_in(key, 11), (N_DP, GROUP_TOKENS, KEY_VALUE_HEADS, CONTEXT_SLOTS, HEAD_DIM), jnp.float32), -6.0, 6.0)
    return (queries, cached_entries)


def draw_queries(key, part):
    return attention_pair(key)[0].astype(jnp.bfloat16)


def draw_key_cache(key, part):
    return attention_pair(key)[1].astype(jnp.bfloat16)


def draw_lengths(key, part):
    drawn_lengths = jax.random.randint(jax.random.fold_in(key, 21), (N_DP * GROUP_TOKENS,), 2, CONTEXT_SLOTS + 1)
    forced_index = jax.random.randint(jax.random.fold_in(key, 22), (), 0, N_DP * GROUP_TOKENS)
    return drawn_lengths.at[forced_index].set(CONTEXT_SLOTS).reshape(N_DP, GROUP_TOKENS)


def draw_residual(key, part):
    entries = jax.random.normal(jax.random.fold_in(key, 41), (BATCH, D), jnp.float32)
    row_scale = loguniform_draw(jax.random.fold_in(key, 42), (BATCH, 1), 0.3, 1.5)
    column_scale = loguniform_draw(jax.random.fold_in(key, 43), (1, D), 0.3, 1.5)
    return jnp.clip(entries * row_scale * column_scale, -8.0, 8.0).astype(jnp.bfloat16)


def draw_routes(key, part):
    busiest = jax.random.randint(jax.random.fold_in(key, 31), (), 0, EXPERTS)
    half_rows = GROUP_TOKENS // 2
    position = jnp.arange(GROUP_TOKENS, dtype=jnp.int32)

    def one_block(block_number):
        block_key = jax.random.fold_in(key, 100 + block_number)
        shuffled = jax.random.permutation(jax.random.fold_in(block_key, 1), GROUP_TOKENS)
        offset = jax.random.randint(jax.random.fold_in(block_key, 2), (), 0, EXPERTS - 1)
        hot_side = jax.random.randint(jax.random.fold_in(block_key, 3), (GROUP_TOKENS,), 0, 2)
        first_slot = jnp.where(position < half_rows, position, half_rows + 2 * (position - half_rows))
        first_other = (offset + first_slot) % (EXPERTS - 1)
        second_other = (offset + first_slot + 1) % (EXPERTS - 1)
        first_other = first_other + (first_other >= busiest).astype(jnp.int32)
        second_other = second_other + (second_other >= busiest).astype(jnp.int32)
        leading = jnp.where(position < half_rows, jnp.where(hot_side == 0, busiest, first_other), first_other)
        trailing = jnp.where(position < half_rows, jnp.where(hot_side == 0, first_other, busiest), second_other)
        route_pair = jnp.stack([leading, trailing], axis=1).astype(jnp.int32)
        return jnp.zeros((GROUP_TOKENS, 2), jnp.int32).at[shuffled].set(route_pair)
    blocks = jax.vmap(one_block)(jnp.arange(N_DP, dtype=jnp.int32))
    return blocks.reshape(BATCH, 2)


def with_spikes(array, key, source, target, parts, factor):
    owner, partner = [(jnp.arange(array.shape[axis_at]) // (array.shape[axis_at] // parts)).reshape([-1 if axis == axis_at else 1 for axis in range(array.ndim)]) for axis_at in (source, target)]
    chosen = jax.random.permutation(key, parts)[partner]
    strong = (owner == chosen) | (owner == (partner + parts // 2) % parts)
    return jnp.where(strong, factor * array, array)


def shard_levels(stream_key, dims, pieces, least, largest):
    def one(dim, shards_of):
        steps = jax.random.uniform(jax.random.fold_in(jax.random.fold_in(stream_key, 6), dim), (shards_of,), jnp.float32, least / len(pieces), largest / len(pieces))
        return jnp.repeat(jnp.exp(steps), dims[dim] // shards_of).reshape((-1,) + (1,) * (len(dims) - dim - 1))

    gain = one(*pieces[0])
    for cut in pieces[1:]:
        gain = gain * one(*cut)
    return gain


def bell_draw(stream_key, shape, scale, reach, split=(), kind=jnp.bfloat16):
    drawn = scale * jax.random.normal(stream_key, shape, jnp.float32)
    if split:
        drawn = drawn * shard_levels(stream_key, shape, split, -0.22, 0.18)
    return jnp.clip(drawn, -reach, reach).astype(kind)


def bell_draw_with(own_key, extent, deviation, reach, shards, heavy, kind=jnp.bfloat16):
    drawn = deviation * jax.random.normal(own_key, extent, jnp.float32)
    if shards:
        drawn = drawn * shard_levels(own_key, extent, shards, -0.22, 0.18)
    return jnp.clip(with_spikes(drawn, jax.random.fold_in(own_key, 3), *heavy), -reach, reach).astype(kind)


def setup_inputs(seed: int = 0) -> dict:
    arg_keys = jax.random.split(jax.random.key(seed), 15)
    queries = draw_queries(jax.random.fold_in(arg_keys[14], 71), 0)
    key_cache = draw_key_cache(jax.random.fold_in(arg_keys[14], 71), 0)
    cached_values = bell_draw(arg_keys[2], (N_DP, GROUP_TOKENS, KEY_VALUE_HEADS, CONTEXT_SLOTS, HEAD_DIM), 2.0, 12.0, ((0, 4), (1, 4), (2, 2)))
    incoming_keys = bell_draw(arg_keys[3], (N_DP, GROUP_TOKENS, KEY_VALUE_HEADS, HEAD_DIM), 2.0, 12.0, ((0, 4), (1, 4), (2, 2)))
    incoming_values = bell_draw(arg_keys[4], (N_DP, GROUP_TOKENS, KEY_VALUE_HEADS, HEAD_DIM), 2.0, 12.0, ((0, 4), (1, 4), (2, 2)))
    lengths = draw_lengths(jax.random.fold_in(arg_keys[14], 71), 0)
    residual = draw_residual(jax.random.fold_in(arg_keys[14], 71), 0)
    out_proj = bell_draw(arg_keys[7], (QUERY_HEADS * HEAD_DIM, D), (QUERY_HEADS * HEAD_DIM) ** -0.5, 0.078125, ((1, 8),))
    norm_gain = jnp.clip(1.0 + 0.18 * jax.random.normal(arg_keys[8], (D,), jnp.float32), 0.1, 1.9)
    router = bell_draw(arg_keys[9], (D, EXPERTS), (D // 9) ** -0.5, 0.21875)
    gate_proj = bell_draw(arg_keys[10], (EXPERTS, D, FFW), D ** -0.5, 0.078125, ((0, 4), (1, 4), (2, 2)))
    up_proj = bell_draw(arg_keys[11], (EXPERTS, D, FFW), D ** -0.5, 0.078125, ((0, 4), (1, 4), (2, 2)))
    down_proj = bell_draw_with(arg_keys[12], (EXPERTS, FFW, D), FFW ** -0.5, 0.09375, ((0, 4), (1, 2), (2, 4)), (1, 2, 4, 2.0))
    routes = draw_routes(jax.random.fold_in(arg_keys[14], 71), 0)
    return dict(queries=queries, key_cache=key_cache, cached_values=cached_values, incoming_keys=incoming_keys, incoming_values=incoming_values, lengths=lengths, residual=residual, out_proj=out_proj, norm_gain=norm_gain, router=router, gate_proj=gate_proj, up_proj=up_proj, down_proj=down_proj, routes=routes)


norm_epsilon = 1e-05

def attend(queries, key_cache, cached_values, incoming_keys, incoming_values, lengths):
    tokens = queries.shape[0]
    query_heads = queries.shape[1]
    head_size = queries.shape[2]
    kv_heads = key_cache.shape[1]
    heads_per_group = query_heads // kv_heads
    logit_scale = 1.0 / math.sqrt(head_size)
    query_head_groups = queries.astype(jnp.float32).reshape(tokens, kv_heads, heads_per_group, head_size)
    cached_entries = jnp.einsum('bkgd,bkpd->bkgp', query_head_groups, key_cache.astype(jnp.float32)) * logit_scale
    new_token_score = jnp.einsum('ncwt,nct->ncw', query_head_groups, incoming_keys.astype(jnp.float32)) * logit_scale
    positions = jnp.arange(key_cache.shape[2], dtype=jnp.int32)
    valid_slots = positions[None, :] < lengths[:, None]
    cached_entries = jnp.where(valid_slots[:, None, None, :], cached_entries, -jnp.inf)
    highest = jnp.maximum(lax.optimization_barrier(jnp.max(cached_entries, axis=-1)), new_token_score)
    cached_exp = jnp.exp(cached_entries - highest[..., None])
    fresh_exp = jnp.exp(new_token_score - highest)
    denominator = lax.optimization_barrier(jnp.sum(cached_exp, axis=-1)) + fresh_exp
    cached_prob = (cached_exp / denominator[..., None]).astype(jnp.bfloat16)
    fresh_prob = (fresh_exp / denominator).astype(jnp.bfloat16)
    gathered = jnp.einsum('bkgp,bkpd->bkgd', cached_prob.astype(jnp.float32), cached_values.astype(jnp.float32))
    gathered = gathered + fresh_prob.astype(jnp.float32)[..., None] * incoming_values.astype(jnp.float32)[:, :, None, :]
    return gathered.reshape(tokens, query_heads * head_size).astype(jnp.bfloat16)

def attend_block(blocks):
    return attend(blocks[0], blocks[1], blocks[2], blocks[3], blocks[4], blocks[5])

def normalize(rows_in, norm_gain):
    values = rows_in.astype(jnp.float32)
    mean_square = lax.optimization_barrier(jnp.mean(values * values, axis=-1, keepdims=True))
    return (values * lax.rsqrt(mean_square + norm_epsilon) * norm_gain).astype(jnp.bfloat16)

def run_expert(packed):
    rows_in, gate_weight, up_weight, down_weight = packed
    gate_pre = jnp.dot(rows_in, gate_weight, preferred_element_type=jnp.float32)
    up_pre = jnp.dot(rows_in, up_weight, preferred_element_type=jnp.float32)
    activated = (jax.nn.silu(gate_pre) * up_pre).astype(jnp.bfloat16)
    return jnp.dot(activated, down_weight, preferred_element_type=jnp.float32).astype(jnp.bfloat16)

def reference(queries, key_cache, cached_values, incoming_keys, incoming_values, lengths, residual, out_proj, norm_gain, router, gate_proj, up_proj, down_proj, routes):
    attended = lax.map(attend_block, (queries, key_cache, cached_values, incoming_keys, incoming_values, lengths))
    attended = attended.reshape(BATCH, QUERY_HEADS * HEAD_DIM)
    projected = jnp.dot(attended, out_proj, preferred_element_type=jnp.float32)
    hidden = (residual.astype(jnp.float32) + projected).astype(jnp.bfloat16)
    normed = normalize(hidden, norm_gain)
    logits = jnp.dot(normed, router, preferred_element_type=jnp.float32)
    chosen = jnp.take_along_axis(logits, routes, axis=1)
    mixing = jax.nn.sigmoid(chosen - chosen[:, ::-1])
    block_routes = routes.reshape(N_DP, 2 * GROUP_TOKENS)
    onehot = (block_routes[..., None] == jnp.arange(EXPERTS, dtype=jnp.int32)[None, None, :]).astype(jnp.int32)
    earlier = jnp.cumsum(onehot, axis=1) - onehot
    target = block_routes * CAP + lax.optimization_barrier(jnp.sum(earlier * onehot, axis=2))
    token_index = jnp.arange(2 * GROUP_TOKENS, dtype=jnp.int32) // 2
    normed_blocks = normed.reshape(N_DP, GROUP_TOKENS, D)

    def fill_block(packed):
        rows_in, slots = packed
        return jnp.zeros((EXPERTS * CAP, D), jnp.bfloat16).at[slots].set(rows_in[token_index])
    buffers = lax.map(fill_block, (normed_blocks, target))
    per_expert = buffers.reshape(N_DP, EXPERTS, CAP, D).transpose(1, 0, 2, 3).reshape(EXPERTS, N_DP * CAP, D)
    outputs = lax.map(run_expert, (per_expert, gate_proj, up_proj, down_proj))
    by_block = outputs.reshape(EXPERTS, N_DP, CAP, D).transpose(1, 0, 2, 3).reshape(N_DP * EXPERTS * CAP, D)
    flat_index = (jnp.arange(N_DP, dtype=jnp.int32)[:, None] * (EXPERTS * CAP) + target).reshape(-1)
    picked = by_block[flat_index].reshape(BATCH, 2, D).astype(jnp.float32)
    combined = lax.optimization_barrier(jnp.sum(mixing[:, :, None] * picked, axis=1))
    return (hidden.astype(jnp.float32) + combined).astype(jnp.bfloat16)
```

```python
import math

import jax
import jax.numpy as jnp
from jax import lax
from jax.sharding import PartitionSpec as P

norm_epsilon = 1e-05


def attend(queries, key_cache, cached_values, incoming_keys, incoming_values, lengths):
    tokens = queries.shape[0]
    query_heads = queries.shape[1]
    head_size = queries.shape[2]
    kv_heads = key_cache.shape[1]
    heads_per_group = query_heads // kv_heads
    logit_scale = 1.0 / math.sqrt(head_size)
    query_head_groups = queries.reshape(tokens, kv_heads, heads_per_group, head_size)
    cached_entries = (
        jnp.einsum(
            "bkgd,bkpd->bkgp", query_head_groups, key_cache, preferred_element_type=jnp.float32
        )
        * logit_scale
    )
    new_token_score = (
        jnp.einsum(
            "ncwt,nct->ncw", query_head_groups, incoming_keys, preferred_element_type=jnp.float32
        )
        * logit_scale
    )
    positions = jnp.arange(key_cache.shape[2], dtype=jnp.int32)
    valid_slots = positions[None, :] < lengths[:, None]
    cached_entries = jnp.where(valid_slots[:, None, None, :], cached_entries, -jnp.inf)
    highest = jnp.maximum(jnp.max(cached_entries, axis=-1), new_token_score)
    cached_exp = jnp.exp(cached_entries - highest[..., None])
    fresh_exp = jnp.exp(new_token_score - highest)
    denominator = jnp.sum(cached_exp, axis=-1) + fresh_exp
    cached_prob = (cached_exp / denominator[..., None]).astype(jnp.bfloat16)
    fresh_prob = (fresh_exp / denominator).astype(jnp.bfloat16)
    gathered = jnp.einsum(
        "bkgp,bkpd->bkgd", cached_prob, cached_values, preferred_element_type=jnp.float32
    )
    gathered = (
        gathered
        + fresh_prob.astype(jnp.float32)[..., None]
        * incoming_values.astype(jnp.float32)[:, :, None, :]
    )
    return gathered.reshape(tokens, query_heads * head_size).astype(jnp.bfloat16)


def normalize(rows_in, norm_gain):
    values = rows_in.astype(jnp.float32)
    mean_square = jnp.mean(values * values, axis=-1, keepdims=True)
    return (values * lax.rsqrt(mean_square + norm_epsilon) * norm_gain).astype(jnp.bfloat16)


def width_share(rows_in):
    share = rows_in.shape[-1] // lax.axis_size("sect")
    return lax.dynamic_slice_in_dim(
        rows_in, lax.axis_index("sect") * share, share, rows_in.ndim - 1
    )


def expert_ffn(arrived, gate_proj, up_proj, down_proj):
    gate_pre = jnp.einsum("esnd,edf->esnf", arrived, gate_proj, preferred_element_type=jnp.float32)
    up_pre = jnp.einsum("esnd,edf->esnf", arrived, up_proj, preferred_element_type=jnp.float32)
    pre = jnp.stack([gate_pre, up_pre]).astype(jnp.bfloat16)
    total = lax.psum_scatter(pre, "sect", scatter_dimension=4, tiled=True).astype(jnp.float32)
    share = (jax.nn.silu(total[0]) * total[1]).astype(jnp.bfloat16)
    activated = lax.all_gather(share, "sect", axis=3, tiled=True)
    partial_out = jnp.einsum(
        "esnf,efd->esnd", activated, down_proj, preferred_element_type=jnp.float32
    )
    return lax.psum_scatter(partial_out.astype(jnp.bfloat16), "tp", scatter_dimension=3, tiled=True)


def per_device(
    queries,
    key_cache,
    cached_values,
    incoming_keys,
    incoming_values,
    lengths,
    residual,
    out_proj,
    norm_gain,
    router,
    gate_proj,
    up_proj,
    down_proj,
    routes,
):
    attended = attend(
        queries[0], key_cache[0], cached_values[0], incoming_keys[0], incoming_values[0], lengths[0]
    )
    seq_local = attended.shape[0]
    tp_count = lax.axis_size("tp")
    head_width = attended.shape[1]
    column_count = out_proj.shape[1]
    weight_split = out_proj.reshape(tp_count, head_width, column_count)
    initial = jnp.zeros((residual.shape[0], column_count), jnp.float32)
    shards = lax.all_gather(attended[None], ("sect", "tp"), axis=0, tiled=True)

    def add_one(counter, current):
        head_block = lax.dynamic_index_in_dim(shards, counter, 0, keepdims=False)
        weight = lax.dynamic_index_in_dim(weight_split, counter % tp_count, 0, keepdims=False)
        product = jnp.dot(head_block, weight, preferred_element_type=jnp.float32)
        row_start = counter // tp_count * seq_local
        earlier = lax.dynamic_slice_in_dim(current, row_start, seq_local, 0)
        return lax.dynamic_update_slice_in_dim(current, earlier + product, row_start, 0)

    projected = lax.fori_loop(0, shards.shape[0], add_one, initial)
    hidden = (residual.astype(jnp.float32) + projected).astype(jnp.bfloat16)
    group_rows = residual.shape[0]
    capacity = group_rows // 2
    expert_count = router.shape[1]
    slot_total = expert_count * capacity
    flat_routes = routes.reshape(-1)
    onehot = (flat_routes[:, None] == jnp.arange(expert_count, dtype=jnp.int32)[None, :]).astype(
        jnp.int32
    )
    earlier_count = jnp.cumsum(onehot, axis=0) - onehot
    target = flat_routes * capacity + jnp.sum(earlier_count * onehot, axis=1)
    matches = target[None, :] == jnp.arange(slot_total, dtype=jnp.int32)[:, None]
    route_token = jnp.arange(flat_routes.shape[0], dtype=jnp.int32) // 2
    slot_token = jnp.sum(jnp.where(matches, route_token[None, :], 0), axis=1)
    slot_used = jnp.any(matches, axis=1)
    full_width = lax.all_gather(hidden, ("sect", "tp"), axis=1, tiled=True)
    normed = normalize(full_width, norm_gain)
    logits = jnp.dot(normed, router, preferred_element_type=jnp.float32)
    chosen = jnp.take_along_axis(logits, routes, axis=1)
    mixing = jax.nn.sigmoid(chosen - chosen[:, ::-1])
    own_share = width_share(normed)
    taken = jnp.take(own_share, slot_token, axis=0)
    outgoing = jnp.where(slot_used[:, None], taken, jnp.zeros((), own_share.dtype)).reshape(
        expert_count, 1, capacity, own_share.shape[1]
    )
    returned = lax.all_to_all(
        expert_ffn(
            lax.all_to_all(outgoing, "dp", split_axis=0, concat_axis=1, tiled=True),
            gate_proj,
            up_proj,
            down_proj,
        ),
        "dp",
        split_axis=1,
        concat_axis=0,
        tiled=True,
    )
    mix_flat = mixing.reshape(-1)
    returned_rows = returned.reshape(slot_total, -1)[target].astype(jnp.float32)
    combined = jnp.sum(
        mix_flat.reshape(group_rows, 2)[:, :, None] * returned_rows.reshape(group_rows, 2, -1),
        axis=1,
    )
    return (hidden.astype(jnp.float32) + combined).astype(jnp.bfloat16)


def solution(mesh):
    placed = (
        P("dp", "sect", "tp", None),
        P("dp", "sect", "tp", None, None),
        P("dp", "sect", "tp", None, None),
        P("dp", "sect", "tp", None),
        P("dp", "sect", "tp", None),
        P("dp", "sect"),
        P("dp", ("sect", "tp")),
        P(None, ("sect", "tp")),
        P(),
        P(),
        P("dp", "sect", "tp"),
        P("dp", "sect", "tp"),
        P("dp", "tp", "sect"),
        P("dp", None),
    )
    return jax.shard_map(
        per_device, mesh=mesh, in_specs=placed, out_specs=P("dp", ("sect", "tp")), check_vma=False
    )
```

```python
import functools
import math

import jax
import jax.numpy as jnp
from jax import lax
from jax.experimental import pallas as pl
from jax.experimental.pallas import tpu as pltpu
from jax.sharding import PartitionSpec as P

norm_epsilon = 1e-05
MESH = pl.DeviceIdType.MESH
TILE = 256


def attend(queries, key_cache, cached_values, incoming_keys, incoming_values, lengths):
    tokens = queries.shape[0]
    query_heads = queries.shape[1]
    head_size = queries.shape[2]
    kv_heads = key_cache.shape[1]
    heads_per_group = query_heads // kv_heads
    logit_scale = 1.0 / math.sqrt(head_size)
    query_head_groups = queries.reshape(tokens, kv_heads, heads_per_group, head_size)
    cached_entries = (
        jnp.einsum(
            "bkgd,bkpd->bkgp", query_head_groups, key_cache, preferred_element_type=jnp.float32
        )
        * logit_scale
    )
    new_token_score = (
        jnp.einsum(
            "ncwt,nct->ncw", query_head_groups, incoming_keys, preferred_element_type=jnp.float32
        )
        * logit_scale
    )
    positions = jnp.arange(key_cache.shape[2], dtype=jnp.int32)
    valid_slots = positions[None, :] < lengths[:, None]
    cached_entries = jnp.where(valid_slots[:, None, None, :], cached_entries, -jnp.inf)
    highest = jnp.maximum(jnp.max(cached_entries, axis=-1), new_token_score)
    cached_exp = jnp.exp(cached_entries - highest[..., None])
    fresh_exp = jnp.exp(new_token_score - highest)
    denominator = jnp.sum(cached_exp, axis=-1) + fresh_exp
    cached_prob = (cached_exp / denominator[..., None]).astype(jnp.bfloat16)
    fresh_prob = (fresh_exp / denominator).astype(jnp.bfloat16)
    gathered = jnp.einsum(
        "bkgp,bkpd->bkgd", cached_prob, cached_values, preferred_element_type=jnp.float32
    )
    gathered = (
        gathered
        + fresh_prob.astype(jnp.float32)[..., None]
        * incoming_values.astype(jnp.float32)[:, :, None, :]
    )
    return gathered.reshape(tokens, query_heads * head_size).astype(jnp.bfloat16)


def normalize(rows_in, norm_gain):
    values = rows_in.astype(jnp.float32)
    mean_square = jnp.mean(values * values, axis=-1, keepdims=True)
    return (values * lax.rsqrt(mean_square + norm_epsilon) * norm_gain).astype(jnp.bfloat16)


def width_share(rows_in):
    share = rows_in.shape[-1] // lax.axis_size("sect")
    return lax.dynamic_slice_in_dim(
        rows_in, lax.axis_index("sect") * share, share, rows_in.ndim - 1
    )


def expert_ffn(arrived, gate_proj, up_proj, down_proj):
    gate_pre = jnp.einsum("esnd,edf->esnf", arrived, gate_proj, preferred_element_type=jnp.float32)
    up_pre = jnp.einsum("esnd,edf->esnf", arrived, up_proj, preferred_element_type=jnp.float32)
    pre = jnp.stack([gate_pre, up_pre]).astype(jnp.bfloat16)
    total = lax.psum_scatter(pre, "sect", scatter_dimension=4, tiled=True).astype(jnp.float32)
    share = (jax.nn.silu(total[0]) * total[1]).astype(jnp.bfloat16)
    activated = lax.all_gather(share, "sect", axis=3, tiled=True)
    partial_out = jnp.einsum(
        "esnf,efd->esnd", activated, down_proj, preferred_element_type=jnp.float32
    )
    return lax.psum_scatter(partial_out.astype(jnp.bfloat16), "tp", scatter_dimension=3, tiled=True)


def layer_kernel(
    sizes,
    attended_ref,
    residual_ref,
    gain_ref,
    router_ref,
    routes_ref,
    out_proj_hbm,
    gate_hbm,
    up_hbm,
    down_hbm,
    out_ref,
    out_w,
    gate_w,
    up_w,
    down_w,
    att_all,
    hidden,
    hit,
    outgoing,
    arrived,
    expert_in,
    square_out,
    square_in,
    pre_out,
    pre_in,
    pre_own,
    act_all,
    down_own,
    pair_out,
    pair_in,
    expert_out,
    returned,
    stat_out,
    stat_in,
    weight_sem,
    att_send,
    att_recv,
    row_send,
    row_recv,
    stat_send,
    stat_recv,
    square_send,
    square_recv,
    pre_send,
    pre_recv,
    act_send,
    act_recv,
    pair_send,
    pair_recv,
    back_send,
    back_recv,
):
    n_sect, n_dp, n_tp = sizes
    sect = lax.axis_index("sect")
    dp = lax.axis_index("dp")
    tp = lax.axis_index("tp")
    group = n_sect * n_tp
    me = sect * n_tp + tp
    f32, bf16 = jnp.float32, jnp.bfloat16

    def flip(value, bits):
        result = value
        bit = 1
        while bit <= bits:
            if bits & bit:
                result = result + bit - 2 * bit * ((value // bit) % 2)
            bit *= 2
        return result

    def in_group(j):
        other = flip(me, j)
        return {"sect": other // n_tp, "dp": dp, "tp": other % n_tp}

    def in_line(i, t):
        return {"sect": sect, "dp": flip(dp, i), "tp": flip(tp, t)}

    loads = []
    for index, (source, target) in enumerate(
        ((out_proj_hbm, out_w), (gate_hbm, gate_w), (up_hbm, up_w), (down_hbm, down_w))
    ):
        rows = source.shape[0] // 4
        for part in range(4):
            pltpu.make_async_copy(
                source.at[pl.ds(part * rows, rows)],
                target.at[pl.ds(part * rows, rows)],
                weight_sem.at[index],
            ).start()
        loads.append(pltpu.make_async_copy(source, target, weight_sem.at[index]))

    barrier = pltpu.get_barrier_semaphore()
    for j in range(1, group):
        pl.semaphore_signal(barrier, inc=1, device_id=in_group(j), device_id_type=MESH)
    for i in range(1, n_dp):
        for t in range(n_tp):
            pl.semaphore_signal(barrier, inc=1, device_id=in_line(i, t), device_id_type=MESH)
    pl.semaphore_wait(barrier, group - 1 + (n_dp - 1) * n_tp)

    seq = attended_ref.shape[0]
    own_rows = pl.ds(pl.multiple_of(sect * seq, seq), seq)
    att_copies = []
    for j in range(1, group):
        copy = pltpu.make_async_remote_copy(
            src_ref=attended_ref,
            dst_ref=att_all.at[tp, own_rows],
            send_sem=att_send.at[j],
            recv_sem=att_recv.at[j],
            device_id=in_group(j),
            device_id_type=MESH,
        )
        copy.start()
        att_copies.append(copy)
    att_all[tp, own_rows, :] = attended_ref[...]

    experts = router_ref.shape[0]
    tokens = routes_ref.shape[1]
    cap = tokens // 2
    slots = experts * cap
    choice = [routes_ref[k : k + 1, :] for k in range(2)]
    expert_ids = lax.broadcasted_iota(jnp.int32, (8, tokens), 0)
    onehot = [jnp.where(expert_ids == choice[k], 1.0, 0.0).astype(f32) for k in range(2)]
    before = jnp.where(
        lax.broadcasted_iota(jnp.int32, (tokens, tokens), 0)
        < lax.broadcasted_iota(jnp.int32, (tokens, tokens), 1),
        1.0,
        0.0,
    ).astype(bf16)
    rank = jnp.dot((onehot[0] + onehot[1]).astype(bf16), before, preferred_element_type=f32)
    slot_ids = lax.broadcasted_iota(jnp.int32, (slots, tokens), 0)
    for k in range(2):
        slot = jnp.sum(rank * onehot[k], axis=0, keepdims=True).astype(jnp.int32)
        hit[k] = jnp.where(slot_ids == choice[k] * cap + slot, 1.0, 0.0).astype(f32)

    loads[0].wait()
    for copy in att_copies:
        copy.wait_recv()

    half = att_all.shape[2]
    width = out_w.shape[1]

    def project(n, carry):
        columns = pl.ds(pl.multiple_of(n * TILE, TILE), TILE)
        total = residual_ref[:, columns].astype(f32)
        for t in range(n_tp):
            total = total + jnp.dot(
                att_all[t], out_w[t * half : (t + 1) * half, columns], preferred_element_type=f32
            )
        hidden[:, columns] = total.astype(bf16)
        return carry

    lax.fori_loop(0, width // TILE, project, 0)

    rows = jnp.dot((hit[0] + hit[1]).astype(bf16), hidden[...], preferred_element_type=f32)
    outgoing[...] = rows.astype(bf16).reshape(experts, cap, width)
    line_rows = pl.ds(pl.multiple_of(dp * cap, cap), cap)
    row_copies = []
    for i in range(n_dp - 1, -1, -1):
        for t in range(n_tp):
            if i == 0 and t == 0:
                continue
            copy = pltpu.make_async_remote_copy(
                src_ref=outgoing.at[flip(dp, i)],
                dst_ref=arrived.at[tp, line_rows],
                send_sem=row_send.at[i * n_tp + t],
                recv_sem=row_recv.at[i * n_tp + t],
                device_id=in_line(i, t),
                device_id_type=MESH,
            )
            copy.start()
            row_copies.append(copy)
    arrived[tp, line_rows, :] = outgoing[dp]

    own = hidden[...].astype(f32)
    scaled = (own * gain_ref[me]).astype(bf16)
    nt = (((1,), (1,)), ((), ()))
    router_part = router_ref[:, pl.ds(pl.multiple_of(me * width, width), width)]
    logit_part = lax.dot_general(router_part, scaled, nt, preferred_element_type=f32)
    square = own * own
    square_high = square.astype(bf16)
    square_low = (square - square_high.astype(f32)).astype(bf16)
    ones = jnp.ones((8, width), bf16)
    square_part = lax.dot_general(
        ones, square_high, nt, preferred_element_type=f32
    ) + lax.dot_general(ones, square_low, nt, preferred_element_type=f32)
    stat_out[...] = jnp.zeros_like(stat_out)
    stat_out[0, 0:experts, 0:tokens] = logit_part
    stat_out[1, :, 0:tokens] = square_part
    stat_copies = []
    for j in range(1, group):
        copy = pltpu.make_async_remote_copy(
            src_ref=stat_out,
            dst_ref=stat_in.at[me],
            send_sem=stat_send.at[j],
            recv_sem=stat_recv.at[j],
            device_id=in_group(j),
            device_id_type=MESH,
        )
        copy.start()
        stat_copies.append(copy)
    stat_in[me] = stat_out[...]

    for copy in row_copies:
        copy.wait_recv()

    total_square = jnp.zeros((arrived.shape[1], 1), f32)
    for t in range(n_tp):
        part = arrived[t].astype(f32)
        total_square = total_square + jnp.sum(part * part, axis=1, keepdims=True)
        expert_in[:, t * width : (t + 1) * width] = (part * gain_ref[sect * n_tp + t]).astype(bf16)
    square_out[...] = jnp.broadcast_to(total_square, square_out.shape)
    square_copies = []
    for j in range(1, n_sect):
        copy = pltpu.make_async_remote_copy(
            src_ref=square_out,
            dst_ref=square_in.at[j],
            send_sem=square_send.at[j],
            recv_sem=square_recv.at[j],
            device_id={"sect": flip(sect, j), "dp": dp, "tp": tp},
            device_id_type=MESH,
        )
        copy.start()
        square_copies.append(copy)

    loads[1].wait()
    loads[2].wait()
    share = act_all.shape[2]
    pre_copies = []
    for j in range(n_sect - 1, -1, -1):
        partner = flip(sect, j)

        def columns_of(n, carry):
            source = pl.ds(pl.multiple_of(partner * share + n * TILE, TILE), TILE)
            target = pl.ds(pl.multiple_of(n * TILE, TILE), TILE)
            for which, weight in enumerate((gate_w, up_w)):
                product = jnp.dot(expert_in[...], weight[:, source], preferred_element_type=f32)
                if j == 0:
                    pre_own[which, :, target] = product
                else:
                    pre_out[j, which, :, target] = product.astype(bf16)
            return carry

        lax.fori_loop(0, share // TILE, columns_of, 0)
        if j:
            copy = pltpu.make_async_remote_copy(
                src_ref=pre_out.at[j],
                dst_ref=pre_in.at[j],
                send_sem=pre_send.at[j],
                recv_sem=pre_recv.at[j],
                device_id={"sect": partner, "dp": dp, "tp": tp},
                device_id_type=MESH,
            )
            copy.start()
            pre_copies.append(copy)

    for copy in square_copies:
        copy.wait_recv()
    summed = square_out[:, 0:1]
    for j in range(1, n_sect):
        summed = summed + square_in[j, :, 0:1]
    features = n_sect * n_tp * width
    scale = lax.rsqrt(summed / features + norm_epsilon)
    for copy in pre_copies:
        copy.wait_recv()
    gate_total, up_total = pre_own[0], pre_own[1]
    for j in range(1, n_sect):
        gate_total = gate_total + pre_in[j, 0].astype(f32)
        up_total = up_total + pre_in[j, 1].astype(f32)
    gate_total = gate_total * scale
    act_all[sect] = (gate_total / (1.0 + jnp.exp(-gate_total)) * (up_total * scale)).astype(bf16)
    act_copies = {}
    for j in range(n_sect - 1, 0, -1):
        copy = pltpu.make_async_remote_copy(
            src_ref=act_all.at[sect],
            dst_ref=act_all.at[sect],
            send_sem=act_send.at[j],
            recv_sem=act_recv.at[j],
            device_id={"sect": flip(sect, j), "dp": dp, "tp": tp},
            device_id_type=MESH,
        )
        copy.start()
        act_copies[j] = copy

    loads[3].wait()
    pair = flip(tp, 1)
    for j in range(n_sect):
        if j:
            act_copies[j].wait_recv()
        partner = flip(sect, j)
        last = j == n_sect - 1
        depth = pl.ds(pl.multiple_of(partner * share, share), share)
        for side in range(2):
            owner = pair if side == 0 else tp

            def down_columns(n, carry):
                source = pl.ds(pl.multiple_of(owner * width + n * TILE, TILE), TILE)
                target = pl.ds(pl.multiple_of(n * TILE, TILE), TILE)
                product = jnp.dot(act_all[partner], down_w[depth, source], preferred_element_type=f32)
                if j:
                    product = product + down_own[side, :, target]
                if last and side == 0:
                    pair_out[:, target] = product.astype(bf16)
                else:
                    down_own[side, :, target] = product
                return carry

            lax.fori_loop(0, width // TILE, down_columns, 0)
            if last and side == 0:
                pair_copy = pltpu.make_async_remote_copy(
                    src_ref=pair_out,
                    dst_ref=pair_in,
                    send_sem=pair_send,
                    recv_sem=pair_recv,
                    device_id={"sect": sect, "dp": dp, "tp": pair},
                    device_id_type=MESH,
                )
                pair_copy.start()
    pair_copy.wait_recv()
    expert_out[...] = (
        (down_own[1] + pair_in[...].astype(f32)).astype(bf16).reshape(n_dp, cap, width)
    )
    back_copies = []
    for i in range(n_dp - 1, 0, -1):
        copy = pltpu.make_async_remote_copy(
            src_ref=expert_out.at[flip(dp, i)],
            dst_ref=returned.at[dp],
            send_sem=back_send.at[i],
            recv_sem=back_recv.at[i],
            device_id=in_line(i, 0),
            device_id_type=MESH,
        )
        copy.start()
        back_copies.append(copy)
    returned[dp] = expert_out[dp]

    for copy in stat_copies:
        copy.wait_recv()
    stats = stat_in[0]
    for j in range(1, group):
        stats = stats + stat_in[j]
    token_scale = lax.rsqrt(stats[1, 0:1, 0:tokens] / features + norm_epsilon)
    logits = stats[0, :, 0:tokens] * token_scale
    chosen = [jnp.sum(logits * onehot[k], axis=0, keepdims=True) for k in range(2)]
    weights = jnp.zeros((slots, tokens), f32)
    for k in range(2):
        mixing = 1.0 / (1.0 + jnp.exp(chosen[1 - k] - chosen[k]))
        weights = weights + hit[k] * mixing
    high = weights.astype(bf16)
    low = (weights - high.astype(f32)).astype(bf16)
    for copy in back_copies:
        copy.wait_recv()
    back = returned[...].reshape(slots, width)
    tn = (((0,), (0,)), ((), ()))
    combined = lax.dot_general(high, back, tn, preferred_element_type=f32) + lax.dot_general(
        low, back, tn, preferred_element_type=f32
    )
    out_ref[...] = (hidden[...].astype(f32) + combined).astype(out_ref.dtype)

    for copy in (
        att_copies + row_copies + stat_copies + square_copies + pre_copies + back_copies
    ):
        copy.wait_send()
    for j in range(1, n_sect):
        act_copies[j].wait_send()
    pair_copy.wait_send()


def fused_layer(
    attended, residual, out_proj, norm_gain, router, gate_proj, up_proj, down_proj, routes
):
    n_sect, n_dp, n_tp = (lax.axis_size(name) for name in ("sect", "dp", "tp"))
    group = n_sect * n_tp
    tokens, width = residual.shape
    experts = router.shape[1]
    cap = tokens // 2
    slots = experts * cap
    rows = n_dp * cap
    share = gate_proj.shape[1] // n_sect
    f32, bf16 = jnp.float32, jnp.bfloat16
    vmem = pl.BlockSpec(memory_space=pltpu.VMEM)
    hbm = pl.BlockSpec(memory_space=pl.ANY)
    dma = pltpu.SemaphoreType.DMA
    buffers = [
        (out_proj.shape, bf16),
        (gate_proj.shape, bf16),
        (up_proj.shape, bf16),
        (down_proj.shape, bf16),
        ((n_tp, tokens, attended.shape[1]), bf16),
        ((tokens, width), bf16),
        ((2, slots, tokens), f32),
        ((experts, cap, width), bf16),
        ((n_tp, rows, width), bf16),
        ((rows, n_tp * width), bf16),
        ((rows, 128), f32),
        ((n_sect, rows, 128), f32),
        ((n_sect, 2, rows, share), bf16),
        ((n_sect, 2, rows, share), bf16),
        ((2, rows, share), f32),
        ((n_sect, rows, share), bf16),
        ((2, rows, width), f32),
        ((rows, width), bf16),
        ((rows, width), bf16),
        ((n_dp, cap, width), bf16),
        ((experts, cap, width), bf16),
        ((2, 8, 128), f32),
        ((group, 2, 8, 128), f32),
    ]
    semaphores = [dma((4,))]
    for count in (group, n_dp * n_tp, group, n_sect, n_sect, n_sect):
        semaphores += [dma((count,)), dma((count,))]
    semaphores += [dma, dma, dma((n_dp,)), dma((n_dp,))]
    return pl.pallas_call(
        functools.partial(layer_kernel, (n_sect, n_dp, n_tp)),
        out_shape=jax.ShapeDtypeStruct((tokens, width), bf16),
        in_specs=[vmem] * 5 + [hbm] * 4,
        out_specs=vmem,
        scratch_shapes=[pltpu.VMEM(shape, kind) for shape, kind in buffers] + semaphores,
        compiler_params=pltpu.CompilerParams(
            collective_id=0, has_side_effects=True, vmem_limit_bytes=61 * 1024 * 1024
        ),
    )(
        attended,
        residual,
        norm_gain.reshape(group, 1, width),
        router.T,
        routes.T,
        out_proj,
        gate_proj,
        up_proj,
        down_proj,
    )


def per_device(
    queries,
    key_cache,
    cached_values,
    incoming_keys,
    incoming_values,
    lengths,
    residual,
    out_proj,
    norm_gain,
    router,
    gate_proj,
    up_proj,
    down_proj,
    routes,
):
    attended = attend(
        queries[0], key_cache[0], cached_values[0], incoming_keys[0], incoming_values[0], lengths[0]
    )
    if lax.axis_size("tp") == 2 and residual.shape[1] % TILE == 0:
        return fused_layer(
            attended,
            residual,
            out_proj,
            norm_gain,
            router,
            gate_proj[0],
            up_proj[0],
            down_proj[0],
            routes,
        )
    seq_local = attended.shape[0]
    tp_count = lax.axis_size("tp")
    head_width = attended.shape[1]
    column_count = out_proj.shape[1]
    weight_split = out_proj.reshape(tp_count, head_width, column_count)
    initial = jnp.zeros((residual.shape[0], column_count), jnp.float32)
    shards = lax.all_gather(attended[None], ("sect", "tp"), axis=0, tiled=True)

    def add_one(counter, current):
        head_block = lax.dynamic_index_in_dim(shards, counter, 0, keepdims=False)
        weight = lax.dynamic_index_in_dim(weight_split, counter % tp_count, 0, keepdims=False)
        product = jnp.dot(head_block, weight, preferred_element_type=jnp.float32)
        row_start = counter // tp_count * seq_local
        earlier = lax.dynamic_slice_in_dim(current, row_start, seq_local, 0)
        return lax.dynamic_update_slice_in_dim(current, earlier + product, row_start, 0)

    projected = lax.fori_loop(0, shards.shape[0], add_one, initial)
    hidden = (residual.astype(jnp.float32) + projected).astype(jnp.bfloat16)
    group_rows = residual.shape[0]
    capacity = group_rows // 2
    expert_count = router.shape[1]
    slot_total = expert_count * capacity
    flat_routes = routes.reshape(-1)
    onehot = (flat_routes[:, None] == jnp.arange(expert_count, dtype=jnp.int32)[None, :]).astype(
        jnp.int32
    )
    earlier_count = jnp.cumsum(onehot, axis=0) - onehot
    target = flat_routes * capacity + jnp.sum(earlier_count * onehot, axis=1)
    matches = target[None, :] == jnp.arange(slot_total, dtype=jnp.int32)[:, None]
    route_token = jnp.arange(flat_routes.shape[0], dtype=jnp.int32) // 2
    slot_token = jnp.sum(jnp.where(matches, route_token[None, :], 0), axis=1)
    slot_used = jnp.any(matches, axis=1)
    full_width = lax.all_gather(hidden, ("sect", "tp"), axis=1, tiled=True)
    normed = normalize(full_width, norm_gain)
    logits = jnp.dot(normed, router, preferred_element_type=jnp.float32)
    chosen = jnp.take_along_axis(logits, routes, axis=1)
    mixing = jax.nn.sigmoid(chosen - chosen[:, ::-1])
    own_share = width_share(normed)
    taken = jnp.take(own_share, slot_token, axis=0)
    outgoing = jnp.where(slot_used[:, None], taken, jnp.zeros((), own_share.dtype)).reshape(
        expert_count, 1, capacity, own_share.shape[1]
    )
    returned = lax.all_to_all(
        expert_ffn(
            lax.all_to_all(outgoing, "dp", split_axis=0, concat_axis=1, tiled=True),
            gate_proj,
            up_proj,
            down_proj,
        ),
        "dp",
        split_axis=1,
        concat_axis=0,
        tiled=True,
    )
    mix_flat = mixing.reshape(-1)
    returned_rows = returned.reshape(slot_total, -1)[target].astype(jnp.float32)
    combined = jnp.sum(
        mix_flat.reshape(group_rows, 2)[:, :, None] * returned_rows.reshape(group_rows, 2, -1),
        axis=1,
    )
    return (hidden.astype(jnp.float32) + combined).astype(jnp.bfloat16)


def solution(mesh):
    placed = (
        P("dp", "sect", "tp", None),
        P("dp", "sect", "tp", None, None),
        P("dp", "sect", "tp", None, None),
        P("dp", "sect", "tp", None),
        P("dp", "sect", "tp", None),
        P("dp", "sect"),
        P("dp", ("sect", "tp")),
        P(None, ("sect", "tp")),
        P(),
        P(),
        P("dp", "sect", "tp"),
        P("dp", "sect", "tp"),
        P("dp", "tp", "sect"),
        P("dp", None),
    )
    return jax.shard_map(
        per_device, mesh=mesh, in_specs=placed, out_specs=P("dp", ("sect", "tp")), check_vma=False
    )
```

```python
import functools
import math

import jax
import jax.numpy as jnp
from jax import lax
from jax.experimental import pallas as pl
from jax.experimental.pallas import tpu as pltpu
from jax.sharding import PartitionSpec as P

norm_epsilon = 1e-05
MESH = pl.DeviceIdType.MESH
TILE = 256


def attend(queries, key_cache, cached_values, incoming_keys, incoming_values, lengths):
    tokens = queries.shape[0]
    query_heads = queries.shape[1]
    head_size = queries.shape[2]
    kv_heads = key_cache.shape[1]
    heads_per_group = query_heads // kv_heads
    logit_scale = 1.0 / math.sqrt(head_size)
    query_head_groups = queries.reshape(tokens, kv_heads, heads_per_group, head_size)
    cached_entries = (
        jnp.einsum(
            "bkgd,bkpd->bkgp", query_head_groups, key_cache, preferred_element_type=jnp.float32
        )
        * logit_scale
    )
    new_token_score = (
        jnp.einsum(
            "ncwt,nct->ncw", query_head_groups, incoming_keys, preferred_element_type=jnp.float32
        )
        * logit_scale
    )
    positions = jnp.arange(key_cache.shape[2], dtype=jnp.int32)
    valid_slots = positions[None, :] < lengths[:, None]
    cached_entries = jnp.where(valid_slots[:, None, None, :], cached_entries, -jnp.inf)
    highest = jnp.maximum(jnp.max(cached_entries, axis=-1), new_token_score)
    cached_exp = jnp.exp(cached_entries - highest[..., None])
    fresh_exp = jnp.exp(new_token_score - highest)
    denominator = jnp.sum(cached_exp, axis=-1) + fresh_exp
    cached_prob = (cached_exp / denominator[..., None]).astype(jnp.bfloat16)
    fresh_prob = (fresh_exp / denominator).astype(jnp.bfloat16)
    gathered = jnp.einsum(
        "bkgp,bkpd->bkgd", cached_prob, cached_values, preferred_element_type=jnp.float32
    )
    gathered = (
        gathered
        + fresh_prob.astype(jnp.float32)[..., None]
        * incoming_values.astype(jnp.float32)[:, :, None, :]
    )
    return gathered.reshape(tokens, query_heads * head_size).astype(jnp.bfloat16)


def normalize(rows_in, norm_gain):
    values = rows_in.astype(jnp.float32)
    mean_square = jnp.mean(values * values, axis=-1, keepdims=True)
    return (values * lax.rsqrt(mean_square + norm_epsilon) * norm_gain).astype(jnp.bfloat16)


def width_share(rows_in):
    share = rows_in.shape[-1] // lax.axis_size("sect")
    return lax.dynamic_slice_in_dim(
        rows_in, lax.axis_index("sect") * share, share, rows_in.ndim - 1
    )


def expert_ffn(arrived, gate_proj, up_proj, down_proj):
    gate_pre = jnp.einsum("esnd,edf->esnf", arrived, gate_proj, preferred_element_type=jnp.float32)
    up_pre = jnp.einsum("esnd,edf->esnf", arrived, up_proj, preferred_element_type=jnp.float32)
    pre = jnp.stack([gate_pre, up_pre]).astype(jnp.bfloat16)
    total = lax.psum_scatter(pre, "sect", scatter_dimension=4, tiled=True).astype(jnp.float32)
    share = (jax.nn.silu(total[0]) * total[1]).astype(jnp.bfloat16)
    activated = lax.all_gather(share, "sect", axis=3, tiled=True)
    partial_out = jnp.einsum(
        "esnf,efd->esnd", activated, down_proj, preferred_element_type=jnp.float32
    )
    return lax.psum_scatter(partial_out.astype(jnp.bfloat16), "tp", scatter_dimension=3, tiled=True)


def layer_kernel(
    sizes,
    attended_ref,
    residual_ref,
    gain_ref,
    router_ref,
    routes_ref,
    out_proj_hbm,
    gate_hbm,
    up_hbm,
    down_hbm,
    out_ref,
    out_w,
    gate_w,
    up_w,
    down_w,
    att_all,
    hidden,
    hit,
    outgoing,
    arrived,
    expert_in,
    square_out,
    square_in,
    pre_out,
    pre_in,
    pre_own,
    pre_pass,
    act_all,
    down_own,
    pair_out,
    pair_in,
    expert_out,
    returned,
    stat_out,
    stat_in,
    weight_sem,
    att_send,
    att_recv,
    row_send,
    row_recv,
    stat_send,
    stat_recv,
    square_send,
    square_recv,
    pre_send,
    pre_recv,
    act_send,
    act_recv,
    pair_send,
    pair_recv,
    back_send,
    back_recv,
):
    n_sect, n_dp, n_tp = sizes
    sect = lax.axis_index("sect")
    dp = lax.axis_index("dp")
    tp = lax.axis_index("tp")
    group = n_sect * n_tp
    me = sect * n_tp + tp
    f32, bf16 = jnp.float32, jnp.bfloat16

    def flip(value, bits):
        result = value
        bit = 1
        while bit <= bits:
            if bits & bit:
                result = result + bit - 2 * bit * ((value // bit) % 2)
            bit *= 2
        return result

    def in_group(j):
        other = flip(me, j)
        return {"sect": other // n_tp, "dp": dp, "tp": other % n_tp}

    def in_sect(j):
        return {"sect": flip(sect, j), "dp": dp, "tp": tp}

    def in_line(i):
        return {"sect": sect, "dp": flip(dp, i), "tp": tp}

    pair = flip(tp, 1)
    in_pair = {"sect": sect, "dp": dp, "tp": pair}

    def send(source, target, send_sem, recv_sem, device):
        copy = pltpu.make_async_remote_copy(
            src_ref=source,
            dst_ref=target,
            send_sem=send_sem,
            recv_sem=recv_sem,
            device_id=device,
            device_id_type=MESH,
        )
        copy.start()
        return copy

    loads = []
    for index, (source, target) in enumerate(
        ((out_proj_hbm, out_w), (gate_hbm, gate_w), (up_hbm, up_w), (down_hbm, down_w))
    ):
        rows = source.shape[0] // 4
        for part in range(4):
            pltpu.make_async_copy(
                source.at[pl.ds(part * rows, rows)],
                target.at[pl.ds(part * rows, rows)],
                weight_sem.at[index],
            ).start()
        loads.append(pltpu.make_async_copy(source, target, weight_sem.at[index]))

    barrier = pltpu.get_barrier_semaphore()
    for j in range(1, group):
        pl.semaphore_signal(barrier, inc=1, device_id=in_group(j), device_id_type=MESH)
    for i in range(1, n_dp):
        pl.semaphore_signal(barrier, inc=1, device_id=in_line(i), device_id_type=MESH)
    pl.semaphore_wait(barrier, group - 1 + n_dp - 1)

    seq = attended_ref.shape[0]

    def seq_rows(j):
        return pl.ds(pl.multiple_of(flip(sect, j) * seq, seq), seq)

    att_copies = {}
    for j in range(n_sect - 1, -1, -1):
        att_copies[j, j == 0] = send(
            attended_ref,
            att_all.at[tp, seq_rows(0)],
            att_send.at[2 * j + (j == 0)],
            att_recv.at[2 * j + (j == 0)],
            in_sect(j) if j else in_pair,
        )
    att_all[tp, seq_rows(0), :] = attended_ref[...]

    experts = router_ref.shape[0]
    tokens = routes_ref.shape[1]
    cap = tokens // 2
    slots = experts * cap
    choice = [routes_ref[k : k + 1, :] for k in range(2)]
    expert_ids = lax.broadcasted_iota(jnp.int32, (8, tokens), 0)
    onehot = [jnp.where(expert_ids == choice[k], 1.0, 0.0).astype(f32) for k in range(2)]
    before = jnp.where(
        lax.broadcasted_iota(jnp.int32, (tokens, tokens), 0)
        < lax.broadcasted_iota(jnp.int32, (tokens, tokens), 1),
        1.0,
        0.0,
    ).astype(bf16)
    rank = jnp.dot((onehot[0] + onehot[1]).astype(bf16), before, preferred_element_type=f32)
    slot_ids = lax.broadcasted_iota(jnp.int32, (slots, tokens), 0)
    for k in range(2):
        slot = jnp.sum(rank * onehot[k], axis=0, keepdims=True).astype(jnp.int32)
        hit[k] = jnp.where(slot_ids == choice[k] * cap + slot, 1.0, 0.0).astype(f32)

    for j in range(1, n_sect):
        att_copies[j, False].wait_recv()
        block = att_all.at[tp, seq_rows(j)]
        att_copies[j, True] = send(
            block, block, att_send.at[2 * j + 1], att_recv.at[2 * j + 1], in_pair
        )
    loads[0].wait()
    for j in range(n_sect):
        att_copies[j, True].wait_recv()

    half = att_all.shape[2]
    width = out_w.shape[1]

    def project(n, carry):
        columns = pl.ds(pl.multiple_of(n * TILE, TILE), TILE)
        total = residual_ref[:, columns].astype(f32)
        for t in range(n_tp):
            total = total + jnp.dot(
                att_all[t], out_w[t * half : (t + 1) * half, columns], preferred_element_type=f32
            )
        hidden[:, columns] = total.astype(bf16)
        return carry

    lax.fori_loop(0, width // TILE, project, 0)

    rows = jnp.dot((hit[0] + hit[1]).astype(bf16), hidden[...], preferred_element_type=f32)
    outgoing[...] = rows.astype(bf16).reshape(experts, cap, width)

    def line_rows(i):
        return pl.ds(pl.multiple_of(flip(dp, i) * cap, cap), cap)

    row_copies = {}
    for i in range(n_dp - 1, -1, -1):
        row_copies[i, i == 0] = send(
            outgoing.at[flip(dp, i)],
            arrived.at[tp, line_rows(0)],
            row_send.at[2 * i + (i == 0)],
            row_recv.at[2 * i + (i == 0)],
            in_line(i) if i else in_pair,
        )
    arrived[tp, line_rows(0), :] = outgoing[dp]

    own = hidden[...].astype(f32)
    scaled = (own * gain_ref[me]).astype(bf16)
    nt = (((1,), (1,)), ((), ()))
    router_part = router_ref[:, pl.ds(pl.multiple_of(me * width, width), width)]
    logit_part = lax.dot_general(router_part, scaled, nt, preferred_element_type=f32)
    square = own * own
    square_high = square.astype(bf16)
    square_low = (square - square_high.astype(f32)).astype(bf16)
    ones = jnp.ones((8, width), bf16)
    square_part = lax.dot_general(
        ones, square_high, nt, preferred_element_type=f32
    ) + lax.dot_general(ones, square_low, nt, preferred_element_type=f32)
    stat_out[...] = jnp.zeros_like(stat_out)
    stat_out[0, 0:experts, 0:tokens] = logit_part
    stat_out[1, :, 0:tokens] = square_part
    stat_copies = []
    for j in range(1, group):
        copy = pltpu.make_async_remote_copy(
            src_ref=stat_out,
            dst_ref=stat_in.at[me],
            send_sem=stat_send.at[j],
            recv_sem=stat_recv.at[j],
            device_id=in_group(j),
            device_id_type=MESH,
        )
        copy.start()
        stat_copies.append(copy)
    stat_in[me] = stat_out[...]

    for i in range(1, n_dp):
        row_copies[i, False].wait_recv()
        block = arrived.at[tp, line_rows(i)]
        row_copies[i, True] = send(
            block, block, row_send.at[2 * i + 1], row_recv.at[2 * i + 1], in_pair
        )

    def take(t):
        part = arrived[t].astype(f32)
        columns = pl.ds(pl.multiple_of(t * width, width), width)
        expert_in[:, columns] = (part * gain_ref[sect * n_tp + t]).astype(bf16)
        return jnp.sum(part * part, axis=1, keepdims=True)

    total_square = take(tp)
    for i in range(n_dp):
        row_copies[i, True].wait_recv()
    total_square = total_square + take(pair)
    square_out[...] = jnp.broadcast_to(total_square, square_out.shape)
    square_copies = [
        send(square_out, square_in.at[j], square_send.at[j], square_recv.at[j], in_sect(j))
        for j in range(1, n_sect)
    ]

    loads[1].wait()
    loads[2].wait()
    share = gate_w.shape[1] // n_sect
    part_width = share // 2
    steps = part_width // TILE
    first, second = (1, 2), (2, 1)

    def products(j, h, store):
        start = flip(sect, j) * share + h * part_width

        def columns_of(n, carry):
            source = pl.ds(pl.multiple_of(start + n * TILE, TILE), TILE)
            target = pl.ds(pl.multiple_of(n * TILE, TILE), TILE)
            for which, weight in enumerate((gate_w, up_w)):
                product = jnp.dot(expert_in[...], weight[:, source], preferred_element_type=f32)
                store(which, target, product)
            return carry

        lax.fori_loop(0, steps, columns_of, 0)

    def pass_on(kind, h, j):
        index = 2 * kind + h
        return send(
            pre_out.at[kind, h],
            pre_in.at[kind, h],
            pre_send.at[index],
            pre_recv.at[index],
            in_sect(j),
        )

    pre_copies = {}
    for kind in range(2):
        for h in range(2):

            def store_out(which, target, product):
                pre_out[kind, h, which, :, target] = product.astype(bf16)

            products(3 if kind == 0 else first[h], h, store_out)
            pre_copies[kind, h] = pass_on(kind, h, first[h])
    for h in range(2):

        def store_pass(which, target, product):
            pre_pass[h, which, :, target] = product

        products(second[h], h, store_pass)
    for h in range(2):
        pre_copies[0, h].wait_recv()

        def add_pass(n, carry):
            target = pl.ds(pl.multiple_of(n * TILE, TILE), TILE)
            for which in range(2):
                total = pre_pass[h, which, :, target] + pre_in[0, h, which, :, target].astype(f32)
                pre_out[2, h, which, :, target] = total.astype(bf16)
            return carry

        lax.fori_loop(0, steps, add_pass, 0)
        pre_copies[2, h] = pass_on(2, h, second[h])
    for h in range(2):

        def store_own(which, target, product):
            pre_own[h, which, :, target] = product

        products(0, h, store_own)

    for copy in square_copies:
        copy.wait_recv()
    summed = square_out[:, 0:1]
    for j in range(1, n_sect):
        summed = summed + square_in[j, :, 0:1]
    features = n_sect * n_tp * width
    scale = lax.rsqrt(summed / features + norm_epsilon)
    act_copies = {}

    def share_act(j, h, block, to):
        index = 2 * j + h
        act_copies[j, h] = send(
            act_all.at[block, h],
            act_all.at[block, h],
            act_send.at[index],
            act_recv.at[index],
            in_sect(to),
        )

    for h in range(2):
        pre_copies[1, h].wait_recv()
        pre_copies[2, h].wait_recv()

        def activate(n, carry):
            target = pl.ds(pl.multiple_of(n * TILE, TILE), TILE)
            sums = []
            for which in range(2):
                total = pre_own[h, which, :, target] + pre_in[1, h, which, :, target].astype(f32)
                total = total + pre_in[2, h, which, :, target].astype(f32)
                sums.append(total * scale)
            active = sums[0] / (1.0 + jnp.exp(-sums[0])) * sums[1]
            act_all[sect, h, :, target] = active.astype(bf16)
            return carry

        lax.fori_loop(0, steps, activate, 0)
        share_act(first[h], h, sect, first[h])
    for h in range(2):
        share_act(second[h], h, sect, second[h])

    loads[3].wait()
    order = ((0, 0), (0, 1), (1, 0), (2, 1), (1, 1), (2, 0), (3, 0), (3, 1))
    for place, (j, h) in enumerate(order):
        partner = flip(sect, j)
        if j:
            act_copies[j, h].wait_recv()
        if (j, h) in ((1, 0), (2, 1)):
            share_act(3, h, partner, second[h])
        last = place == len(order) - 1
        depth = pl.ds(pl.multiple_of(partner * share + h * part_width, part_width), part_width)
        for side in range(2):
            owner = pair if side == 0 else tp

            def down_columns(n, carry):
                source = pl.ds(pl.multiple_of(owner * width + n * TILE, TILE), TILE)
                target = pl.ds(pl.multiple_of(n * TILE, TILE), TILE)
                product = jnp.dot(
                    act_all[partner, h], down_w[depth, source], preferred_element_type=f32
                )
                if place:
                    product = product + down_own[side, :, target]
                if last and side == 0:
                    pair_out[:, target] = product.astype(bf16)
                else:
                    down_own[side, :, target] = product
                return carry

            lax.fori_loop(0, width // TILE, down_columns, 0)
            if last and side == 0:
                pair_copy = send(pair_out, pair_in, pair_send, pair_recv, in_pair)
    pair_copy.wait_recv()
    expert_out[...] = (
        (down_own[1] + pair_in[...].astype(f32)).astype(bf16).reshape(n_dp, cap, width)
    )
    back_copies = [
        send(
            expert_out.at[flip(dp, i)],
            returned.at[dp],
            back_send.at[i],
            back_recv.at[i],
            in_line(i),
        )
        for i in range(n_dp - 1, 0, -1)
    ]
    returned[dp] = expert_out[dp]

    for copy in stat_copies:
        copy.wait_recv()
    stats = stat_in[0]
    for j in range(1, group):
        stats = stats + stat_in[j]
    token_scale = lax.rsqrt(stats[1, 0:1, 0:tokens] / features + norm_epsilon)
    logits = stats[0, :, 0:tokens] * token_scale
    chosen = [jnp.sum(logits * onehot[k], axis=0, keepdims=True) for k in range(2)]
    weights = jnp.zeros((slots, tokens), f32)
    for k in range(2):
        mixing = 1.0 / (1.0 + jnp.exp(chosen[1 - k] - chosen[k]))
        weights = weights + hit[k] * mixing
    high = weights.astype(bf16)
    low = (weights - high.astype(f32)).astype(bf16)
    for copy in back_copies:
        copy.wait_recv()
    back = returned[...].reshape(slots, width)
    tn = (((0,), (0,)), ((), ()))
    combined = lax.dot_general(high, back, tn, preferred_element_type=f32) + lax.dot_general(
        low, back, tn, preferred_element_type=f32
    )
    out_ref[...] = (hidden[...].astype(f32) + combined).astype(out_ref.dtype)

    for copies in (att_copies, row_copies, pre_copies, act_copies):
        for copy in copies.values():
            copy.wait_send()
    for copy in stat_copies + square_copies + back_copies + [pair_copy]:
        copy.wait_send()


def fused_layer(
    attended, residual, out_proj, norm_gain, router, gate_proj, up_proj, down_proj, routes
):
    n_sect, n_dp, n_tp = (lax.axis_size(name) for name in ("sect", "dp", "tp"))
    group = n_sect * n_tp
    tokens, width = residual.shape
    experts = router.shape[1]
    cap = tokens // 2
    slots = experts * cap
    rows = n_dp * cap
    share = gate_proj.shape[1] // n_sect
    f32, bf16 = jnp.float32, jnp.bfloat16
    vmem = pl.BlockSpec(memory_space=pltpu.VMEM)
    hbm = pl.BlockSpec(memory_space=pl.ANY)
    dma = pltpu.SemaphoreType.DMA
    buffers = [
        (out_proj.shape, bf16),
        (gate_proj.shape, bf16),
        (up_proj.shape, bf16),
        (down_proj.shape, bf16),
        ((n_tp, tokens, attended.shape[1]), bf16),
        ((tokens, width), bf16),
        ((2, slots, tokens), f32),
        ((experts, cap, width), bf16),
        ((n_tp, rows, width), bf16),
        ((rows, n_tp * width), bf16),
        ((rows, 128), f32),
        ((n_sect, rows, 128), f32),
        ((3, 2, 2, rows, share // 2), bf16),
        ((3, 2, 2, rows, share // 2), bf16),
        ((2, 2, rows, share // 2), f32),
        ((2, 2, rows, share // 2), f32),
        ((n_sect, 2, rows, share // 2), bf16),
        ((2, rows, width), f32),
        ((rows, width), bf16),
        ((rows, width), bf16),
        ((n_dp, cap, width), bf16),
        ((experts, cap, width), bf16),
        ((2, 8, 128), f32),
        ((group, 2, 8, 128), f32),
    ]
    semaphores = [dma((4,))]
    for count in (2 * n_sect, 2 * n_dp, group, n_sect, 6, 2 * n_sect):
        semaphores += [dma((count,)), dma((count,))]
    semaphores += [dma, dma, dma((n_dp,)), dma((n_dp,))]
    return pl.pallas_call(
        functools.partial(layer_kernel, (n_sect, n_dp, n_tp)),
        out_shape=jax.ShapeDtypeStruct((tokens, width), bf16),
        in_specs=[vmem] * 5 + [hbm] * 4,
        out_specs=vmem,
        scratch_shapes=[pltpu.VMEM(shape, kind) for shape, kind in buffers] + semaphores,
        compiler_params=pltpu.CompilerParams(
            collective_id=0, has_side_effects=True, vmem_limit_bytes=61 * 1024 * 1024
        ),
    )(
        attended,
        residual,
        norm_gain.reshape(group, 1, width),
        router.T,
        routes.T,
        out_proj,
        gate_proj,
        up_proj,
        down_proj,
    )


def per_device(
    queries,
    key_cache,
    cached_values,
    incoming_keys,
    incoming_values,
    lengths,
    residual,
    out_proj,
    norm_gain,
    router,
    gate_proj,
    up_proj,
    down_proj,
    routes,
):
    attended = attend(
        queries[0], key_cache[0], cached_values[0], incoming_keys[0], incoming_values[0], lengths[0]
    )
    fits = lax.axis_size("sect") == 4 and lax.axis_size("tp") == 2
    if fits and residual.shape[1] % TILE == 0:
        return fused_layer(
            attended,
            residual,
            out_proj,
            norm_gain,
            router,
            gate_proj[0],
            up_proj[0],
            down_proj[0],
            routes,
        )
    seq_local = attended.shape[0]
    tp_count = lax.axis_size("tp")
    head_width = attended.shape[1]
    column_count = out_proj.shape[1]
    weight_split = out_proj.reshape(tp_count, head_width, column_count)
    initial = jnp.zeros((residual.shape[0], column_count), jnp.float32)
    shards = lax.all_gather(attended[None], ("sect", "tp"), axis=0, tiled=True)

    def add_one(counter, current):
        head_block = lax.dynamic_index_in_dim(shards, counter, 0, keepdims=False)
        weight = lax.dynamic_index_in_dim(weight_split, counter % tp_count, 0, keepdims=False)
        product = jnp.dot(head_block, weight, preferred_element_type=jnp.float32)
        row_start = counter // tp_count * seq_local
        earlier = lax.dynamic_slice_in_dim(current, row_start, seq_local, 0)
        return lax.dynamic_update_slice_in_dim(current, earlier + product, row_start, 0)

    projected = lax.fori_loop(0, shards.shape[0], add_one, initial)
    hidden = (residual.astype(jnp.float32) + projected).astype(jnp.bfloat16)
    group_rows = residual.shape[0]
    capacity = group_rows // 2
    expert_count = router.shape[1]
    slot_total = expert_count * capacity
    flat_routes = routes.reshape(-1)
    onehot = (flat_routes[:, None] == jnp.arange(expert_count, dtype=jnp.int32)[None, :]).astype(
        jnp.int32
    )
    earlier_count = jnp.cumsum(onehot, axis=0) - onehot
    target = flat_routes * capacity + jnp.sum(earlier_count * onehot, axis=1)
    matches = target[None, :] == jnp.arange(slot_total, dtype=jnp.int32)[:, None]
    route_token = jnp.arange(flat_routes.shape[0], dtype=jnp.int32) // 2
    slot_token = jnp.sum(jnp.where(matches, route_token[None, :], 0), axis=1)
    slot_used = jnp.any(matches, axis=1)
    full_width = lax.all_gather(hidden, ("sect", "tp"), axis=1, tiled=True)
    normed = normalize(full_width, norm_gain)
    logits = jnp.dot(normed, router, preferred_element_type=jnp.float32)
    chosen = jnp.take_along_axis(logits, routes, axis=1)
    mixing = jax.nn.sigmoid(chosen - chosen[:, ::-1])
    own_share = width_share(normed)
    taken = jnp.take(own_share, slot_token, axis=0)
    outgoing = jnp.where(slot_used[:, None], taken, jnp.zeros((), own_share.dtype)).reshape(
        expert_count, 1, capacity, own_share.shape[1]
    )
    returned = lax.all_to_all(
        expert_ffn(
            lax.all_to_all(outgoing, "dp", split_axis=0, concat_axis=1, tiled=True),
            gate_proj,
            up_proj,
            down_proj,
        ),
        "dp",
        split_axis=1,
        concat_axis=0,
        tiled=True,
    )
    mix_flat = mixing.reshape(-1)
    returned_rows = returned.reshape(slot_total, -1)[target].astype(jnp.float32)
    combined = jnp.sum(
        mix_flat.reshape(group_rows, 2)[:, :, None] * returned_rows.reshape(group_rows, 2, -1),
        axis=1,
    )
    return (hidden.astype(jnp.float32) + combined).astype(jnp.bfloat16)


def solution(mesh):
    placed = (
        P("dp", "sect", "tp", None),
        P("dp", "sect", "tp", None, None),
        P("dp", "sect", "tp", None, None),
        P("dp", "sect", "tp", None),
        P("dp", "sect", "tp", None),
        P("dp", "sect"),
        P("dp", ("sect", "tp")),
        P(None, ("sect", "tp")),
        P(),
        P(),
        P("dp", "sect", "tp"),
        P("dp", "sect", "tp"),
        P("dp", "tp", "sect"),
        P("dp", None),
    )
    return jax.shard_map(
        per_device, mesh=mesh, in_specs=placed, out_specs=P("dp", ("sect", "tp")), check_vma=False
    )
```

```python
import functools
import math

import jax
import jax.numpy as jnp
from jax import lax
from jax.experimental import pallas as pl
from jax.experimental.pallas import tpu as pltpu
from jax.sharding import PartitionSpec as P

norm_epsilon = 1e-05
MESH = pl.DeviceIdType.MESH
TILE = 256


def attend(queries, key_cache, cached_values, incoming_keys, incoming_values, lengths):
    tokens = queries.shape[0]
    query_heads = queries.shape[1]
    head_size = queries.shape[2]
    kv_heads = key_cache.shape[1]
    heads_per_group = query_heads // kv_heads
    logit_scale = 1.0 / math.sqrt(head_size)
    query_head_groups = queries.reshape(tokens, kv_heads, heads_per_group, head_size)
    cached_entries = (
        jnp.einsum(
            "bkgd,bkpd->bkgp", query_head_groups, key_cache, preferred_element_type=jnp.float32
        )
        * logit_scale
    )
    new_token_score = (
        jnp.einsum(
            "ncwt,nct->ncw", query_head_groups, incoming_keys, preferred_element_type=jnp.float32
        )
        * logit_scale
    )
    positions = jnp.arange(key_cache.shape[2], dtype=jnp.int32)
    valid_slots = positions[None, :] < lengths[:, None]
    cached_entries = jnp.where(valid_slots[:, None, None, :], cached_entries, -jnp.inf)
    highest = jnp.maximum(jnp.max(cached_entries, axis=-1), new_token_score)
    cached_exp = jnp.exp(cached_entries - highest[..., None])
    fresh_exp = jnp.exp(new_token_score - highest)
    denominator = jnp.sum(cached_exp, axis=-1) + fresh_exp
    cached_prob = (cached_exp / denominator[..., None]).astype(jnp.bfloat16)
    fresh_prob = (fresh_exp / denominator).astype(jnp.bfloat16)
    gathered = jnp.einsum(
        "bkgp,bkpd->bkgd", cached_prob, cached_values, preferred_element_type=jnp.float32
    )
    gathered = (
        gathered
        + fresh_prob.astype(jnp.float32)[..., None]
        * incoming_values.astype(jnp.float32)[:, :, None, :]
    )
    return gathered.reshape(tokens, query_heads * head_size).astype(jnp.bfloat16)


def normalize(rows_in, norm_gain):
    values = rows_in.astype(jnp.float32)
    mean_square = jnp.mean(values * values, axis=-1, keepdims=True)
    return (values * lax.rsqrt(mean_square + norm_epsilon) * norm_gain).astype(jnp.bfloat16)


def width_share(rows_in):
    share = rows_in.shape[-1] // lax.axis_size("sect")
    return lax.dynamic_slice_in_dim(
        rows_in, lax.axis_index("sect") * share, share, rows_in.ndim - 1
    )


def expert_ffn(arrived, gate_proj, up_proj, down_proj):
    gate_pre = jnp.einsum("esnd,edf->esnf", arrived, gate_proj, preferred_element_type=jnp.float32)
    up_pre = jnp.einsum("esnd,edf->esnf", arrived, up_proj, preferred_element_type=jnp.float32)
    pre = jnp.stack([gate_pre, up_pre]).astype(jnp.bfloat16)
    total = lax.psum_scatter(pre, "sect", scatter_dimension=4, tiled=True).astype(jnp.float32)
    share = (jax.nn.silu(total[0]) * total[1]).astype(jnp.bfloat16)
    activated = lax.all_gather(share, "sect", axis=3, tiled=True)
    partial_out = jnp.einsum(
        "esnf,efd->esnd", activated, down_proj, preferred_element_type=jnp.float32
    )
    return lax.psum_scatter(partial_out.astype(jnp.bfloat16), "tp", scatter_dimension=3, tiled=True)


def layer_kernel(
    sizes,
    queries_ref,
    fresh_keys_ref,
    fresh_values_ref,
    lengths_ref,
    residual_ref,
    gain_ref,
    router_ref,
    routes_ref,
    keys_hbm,
    values_hbm,
    out_proj_hbm,
    gate_hbm,
    up_hbm,
    down_hbm,
    out_ref,
    keys,
    values,
    by_token,
    attended,
    out_w,
    gate_w,
    up_w,
    down_w,
    att_all,
    hidden,
    hit,
    outgoing,
    arrived,
    expert_in,
    square_out,
    square_in,
    pre_out,
    pre_in,
    pre_own,
    act_all,
    down_own,
    pair_out,
    pair_in,
    expert_out,
    returned,
    stat_out,
    stat_in,
    cache_sem,
    weight_sem,
    att_send,
    att_recv,
    row_send,
    row_recv,
    stat_send,
    stat_recv,
    square_send,
    square_recv,
    pre_send,
    pre_recv,
    act_send,
    act_recv,
    pair_send,
    pair_recv,
    back_send,
    back_recv,
):
    n_sect, n_dp, n_tp = sizes
    sect = lax.axis_index("sect")
    dp = lax.axis_index("dp")
    tp = lax.axis_index("tp")
    group = n_sect * n_tp
    me = sect * n_tp + tp
    f32, bf16 = jnp.float32, jnp.bfloat16

    def flip(value, bits):
        result = value
        bit = 1
        while bit <= bits:
            if bits & bit:
                result = result + bit - 2 * bit * ((value // bit) % 2)
            bit *= 2
        return result

    def in_group(j):
        other = flip(me, j)
        return {"sect": other // n_tp, "dp": dp, "tp": other % n_tp}

    def in_sect(j):
        return {"sect": flip(sect, j), "dp": dp, "tp": tp}

    def in_line(i):
        return {"sect": sect, "dp": flip(dp, i), "tp": tp}

    pair = flip(tp, 1)
    in_pair = {"sect": sect, "dp": dp, "tp": pair}

    def send(source, target, send_sem, recv_sem, device):
        copy = pltpu.make_async_remote_copy(
            src_ref=source,
            dst_ref=target,
            send_sem=send_sem,
            recv_sem=recv_sem,
            device_id=device,
            device_id_type=MESH,
        )
        copy.start()
        return copy

    seq, query_heads, head_size = queries_ref.shape
    pieces = 4
    cache_loads = []
    for piece in range(pieces):
        span = pl.ds(piece * (seq // pieces), seq // pieces)
        for which, (source, target) in enumerate(((keys_hbm, keys), (values_hbm, values))):
            copy = pltpu.make_async_copy(
                source.at[span], target.at[span], cache_sem.at[which, piece]
            )
            copy.start()
            cache_loads.append(copy)
    loads = []
    for index, (source, target) in enumerate(
        ((out_proj_hbm, out_w), (gate_hbm, gate_w), (up_hbm, up_w), (down_hbm, down_w))
    ):
        rows = source.shape[0] // 4
        for part in range(4):
            pltpu.make_async_copy(
                source.at[pl.ds(part * rows, rows)],
                target.at[pl.ds(part * rows, rows)],
                weight_sem.at[index],
            ).start()
        loads.append(pltpu.make_async_copy(source, target, weight_sem.at[index]))

    barrier = pltpu.get_barrier_semaphore()
    for j in range(1, group):
        pl.semaphore_signal(barrier, inc=1, device_id=in_group(j), device_id_type=MESH)
    for i in range(1, n_dp):
        pl.semaphore_signal(barrier, inc=1, device_id=in_line(i), device_id_type=MESH)

    kv_heads, context = keys.shape[1], keys.shape[2]
    per_group = query_heads // kv_heads
    every = kv_heads * context
    nt = (((1,), (1,)), ((), ()))
    head_of_row = lax.broadcasted_iota(jnp.int32, (query_heads, every), 0) // per_group
    slot_of_column = lax.broadcasted_iota(jnp.int32, (query_heads, every), 1)
    head_of_column = slot_of_column // context
    position = jnp.where(
        head_of_row == head_of_column, slot_of_column - head_of_column * context, context
    )
    fresh_same = (
        lax.broadcasted_iota(jnp.int32, (query_heads, kv_heads), 0) // per_group
    ) == lax.broadcasted_iota(jnp.int32, (query_heads, kv_heads), 1)
    logit_scale = 1.0 / math.sqrt(head_size)

    def attend_token(b):
        query = queries_ref[b]
        scores = lax.dot_general(
            query, keys[b].reshape(every, head_size), nt, preferred_element_type=f32
        )
        fresh = lax.dot_general(query, fresh_keys_ref[b], nt, preferred_element_type=f32)
        scores = jnp.where(position < lengths_ref[0, b], scores * logit_scale, -jnp.inf)
        fresh = jnp.where(fresh_same, fresh * logit_scale, -jnp.inf)
        highest = jnp.maximum(
            jnp.max(scores, axis=1, keepdims=True), jnp.max(fresh, axis=1, keepdims=True)
        )
        scores = jnp.exp(scores - highest)
        fresh = jnp.exp(fresh - highest)
        total = jnp.sum(scores, axis=1, keepdims=True) + jnp.sum(fresh, axis=1, keepdims=True)
        inverse = 1.0 / total
        probs = (scores * inverse).astype(bf16)
        fresh_probs = (fresh * inverse).astype(bf16)
        mixed = jnp.dot(probs, values[b].reshape(every, head_size), preferred_element_type=f32)
        fresh_part = jnp.dot(fresh_probs, fresh_values_ref[b], preferred_element_type=f32)
        return mixed + fresh_part

    step = seq // pieces
    for piece in range(pieces):
        cache_loads[2 * piece].wait()
        cache_loads[2 * piece + 1].wait()

        def attend_step(b, carry):
            by_token[b] = attend_token(b)
            return carry

        lax.fori_loop(piece * step, (piece + 1) * step, attend_step, 0, unroll=True)
    count = seq * query_heads
    row = lax.broadcasted_iota(jnp.int32, (count, count), 0)
    column = lax.broadcasted_iota(jnp.int32, (count, count), 1)
    source = (row % seq) * query_heads + row // seq
    order = jnp.where(column == source, 1.0, 0.0).astype(bf16)
    rows_by_token = by_token[...].reshape(count, head_size).astype(bf16)
    attended[...] = (
        jnp.dot(order, rows_by_token, preferred_element_type=f32)
        .astype(bf16)
        .reshape(query_heads, seq, head_size)
    )
    pl.semaphore_wait(barrier, group - 1 + n_dp - 1)


    def seq_rows(j):
        return pl.ds(pl.multiple_of(flip(sect, j) * seq, seq), seq)

    att_copies = {}
    for j in range(n_sect - 1, -1, -1):
        att_copies[j, j == 0] = send(
            attended,
            att_all.at[tp, :, seq_rows(0)],
            att_send.at[2 * j + (j == 0)],
            att_recv.at[2 * j + (j == 0)],
            in_sect(j) if j else in_pair,
        )
    att_all[tp, :, seq_rows(0), :] = attended[...]

    experts = router_ref.shape[0]
    tokens = routes_ref.shape[1]
    cap = tokens // 2
    slots = experts * cap
    choice = [routes_ref[k : k + 1, :] for k in range(2)]
    expert_ids = lax.broadcasted_iota(jnp.int32, (8, tokens), 0)
    onehot = [jnp.where(expert_ids == choice[k], 1.0, 0.0).astype(f32) for k in range(2)]
    before = jnp.where(
        lax.broadcasted_iota(jnp.int32, (tokens, tokens), 0)
        < lax.broadcasted_iota(jnp.int32, (tokens, tokens), 1),
        1.0,
        0.0,
    ).astype(bf16)
    rank = jnp.dot((onehot[0] + onehot[1]).astype(bf16), before, preferred_element_type=f32)
    slot_ids = lax.broadcasted_iota(jnp.int32, (slots, tokens), 0)
    for k in range(2):
        slot = jnp.sum(rank * onehot[k], axis=0, keepdims=True).astype(jnp.int32)
        hit[k] = jnp.where(slot_ids == choice[k] * cap + slot, 1.0, 0.0).astype(f32)

    for j in range(1, n_sect):
        att_copies[j, False].wait_recv()
        block = att_all.at[tp, :, seq_rows(j)]
        att_copies[j, True] = send(
            block, block, att_send.at[2 * j + 1], att_recv.at[2 * j + 1], in_pair
        )
    loads[0].wait()
    for j in range(n_sect):
        att_copies[j, True].wait_recv()

    half = query_heads * head_size
    width = out_w.shape[1]

    def project(n, carry):
        columns = pl.ds(pl.multiple_of(n * TILE, TILE), TILE)
        total = residual_ref[:, columns].astype(f32)
        for t in range(n_tp):
            heads = jnp.concatenate([att_all[t, head] for head in range(query_heads)], axis=1)
            total = total + jnp.dot(
                heads, out_w[t * half : (t + 1) * half, columns], preferred_element_type=f32
            )
        hidden[:, columns] = total.astype(bf16)
        return carry

    lax.fori_loop(0, width // TILE, project, 0)

    rows = jnp.dot((hit[0] + hit[1]).astype(bf16), hidden[...], preferred_element_type=f32)
    outgoing[...] = rows.astype(bf16).reshape(experts, cap, width)

    def line_rows(i):
        return pl.ds(pl.multiple_of(flip(dp, i) * cap, cap), cap)

    row_copies = {}
    for i in range(n_dp - 1, -1, -1):
        row_copies[i, i == 0] = send(
            outgoing.at[flip(dp, i)],
            arrived.at[tp, line_rows(0)],
            row_send.at[2 * i + (i == 0)],
            row_recv.at[2 * i + (i == 0)],
            in_line(i) if i else in_pair,
        )
    arrived[tp, line_rows(0), :] = outgoing[dp]

    own = hidden[...].astype(f32)
    scaled = (own * gain_ref[me]).astype(bf16)
    nt = (((1,), (1,)), ((), ()))
    router_part = router_ref[:, pl.ds(pl.multiple_of(me * width, width), width)]
    logit_part = lax.dot_general(router_part, scaled, nt, preferred_element_type=f32)
    square = own * own
    square_high = square.astype(bf16)
    square_low = (square - square_high.astype(f32)).astype(bf16)
    ones = jnp.ones((8, width), bf16)
    square_part = lax.dot_general(
        ones, square_high, nt, preferred_element_type=f32
    ) + lax.dot_general(ones, square_low, nt, preferred_element_type=f32)
    stat_out[...] = jnp.zeros_like(stat_out)
    stat_out[0, 0:experts, 0:tokens] = logit_part
    stat_out[1, :, 0:tokens] = square_part
    stat_copies = []
    for j in range(1, group):
        copy = pltpu.make_async_remote_copy(
            src_ref=stat_out,
            dst_ref=stat_in.at[me],
            send_sem=stat_send.at[j],
            recv_sem=stat_recv.at[j],
            device_id=in_group(j),
            device_id_type=MESH,
        )
        copy.start()
        stat_copies.append(copy)
    stat_in[me] = stat_out[...]

    for i in range(1, n_dp):
        row_copies[i, False].wait_recv()
        block = arrived.at[tp, line_rows(i)]
        row_copies[i, True] = send(
            block, block, row_send.at[2 * i + 1], row_recv.at[2 * i + 1], in_pair
        )

    def take(t):
        part = arrived[t].astype(f32)
        columns = pl.ds(pl.multiple_of(t * width, width), width)
        expert_in[:, columns] = (part * gain_ref[sect * n_tp + t]).astype(bf16)
        return jnp.sum(part * part, axis=1, keepdims=True)

    total_square = take(tp)
    for i in range(n_dp):
        row_copies[i, True].wait_recv()
    total_square = total_square + take(pair)
    square_out[...] = jnp.broadcast_to(total_square, square_out.shape)
    square_copies = [
        send(square_out, square_in.at[j], square_send.at[j], square_recv.at[j], in_sect(j))
        for j in range(1, n_sect)
    ]

    loads[1].wait()
    loads[2].wait()
    share = gate_w.shape[1] // n_sect
    part_width = share // 2
    steps = part_width // TILE
    first, second = (1, 2), (2, 1)

    def products(j, h, store):
        start = flip(sect, j) * share + h * part_width

        def columns_of(n, carry):
            source = pl.ds(pl.multiple_of(start + n * TILE, TILE), TILE)
            target = pl.ds(pl.multiple_of(n * TILE, TILE), TILE)
            for which, weight in enumerate((gate_w, up_w)):
                product = jnp.dot(expert_in[...], weight[:, source], preferred_element_type=f32)
                store(which, target, product)
            return carry

        lax.fori_loop(0, steps, columns_of, 0)

    def pass_on(kind, h, j):
        index = 2 * kind + h
        return send(
            pre_out.at[kind, h],
            pre_in.at[kind, h],
            pre_send.at[index],
            pre_recv.at[index],
            in_sect(j),
        )

    pre_copies = {}
    for kind in range(2):
        for h in range(2):

            def store_out(which, target, product):
                pre_out[kind, h, which, :, target] = product.astype(bf16)

            products(3 if kind == 0 else first[h], h, store_out)
            pre_copies[kind, h] = pass_on(kind, h, first[h])
    for h in range(2):

        def store_pass(which, target, product):
            pre_own[h, which, :, target] = product

        products(second[h], h, store_pass)
    for h in range(2):
        pre_copies[0, h].wait_recv()

        def add_pass(n, carry):
            target = pl.ds(pl.multiple_of(n * TILE, TILE), TILE)
            for which in range(2):
                total = pre_own[h, which, :, target] + pre_in[0, h, which, :, target].astype(f32)
                pre_out[2, h, which, :, target] = total.astype(bf16)
            return carry

        lax.fori_loop(0, steps, add_pass, 0)
        pre_copies[2, h] = pass_on(2, h, second[h])
    for h in range(2):

        def store_own(which, target, product):
            pre_own[h, which, :, target] = product

        products(0, h, store_own)

    for copy in square_copies:
        copy.wait_recv()
    summed = square_out[:, 0:1]
    for j in range(1, n_sect):
        summed = summed + square_in[j, :, 0:1]
    features = n_sect * n_tp * width
    scale = lax.rsqrt(summed / features + norm_epsilon)
    act_copies = {}

    def share_act(j, h, block, to):
        index = 2 * j + h
        act_copies[j, h] = send(
            act_all.at[block, h],
            act_all.at[block, h],
            act_send.at[index],
            act_recv.at[index],
            in_sect(to),
        )

    for h in range(2):
        pre_copies[1, h].wait_recv()
        pre_copies[2, h].wait_recv()

        def activate(n, carry):
            target = pl.ds(pl.multiple_of(n * TILE, TILE), TILE)
            sums = []
            for which in range(2):
                total = pre_own[h, which, :, target] + pre_in[1, h, which, :, target].astype(f32)
                total = total + pre_in[2, h, which, :, target].astype(f32)
                sums.append(total * scale)
            active = sums[0] / (1.0 + jnp.exp(-sums[0])) * sums[1]
            act_all[sect, h, :, target] = active.astype(bf16)
            return carry

        lax.fori_loop(0, steps, activate, 0)
        share_act(first[h], h, sect, first[h])
    for h in range(2):
        share_act(second[h], h, sect, second[h])

    loads[3].wait()
    order = ((0, 0), (0, 1), (1, 0), (2, 1), (1, 1), (2, 0), (3, 0), (3, 1))
    for place, (j, h) in enumerate(order):
        partner = flip(sect, j)
        if j:
            act_copies[j, h].wait_recv()
        if (j, h) in ((1, 0), (2, 1)):
            share_act(3, h, partner, second[h])
        last = place == len(order) - 1
        depth = pl.ds(pl.multiple_of(partner * share + h * part_width, part_width), part_width)
        for side in range(2):
            owner = pair if side == 0 else tp

            def down_columns(n, carry):
                source = pl.ds(pl.multiple_of(owner * width + n * TILE, TILE), TILE)
                target = pl.ds(pl.multiple_of(n * TILE, TILE), TILE)
                product = jnp.dot(
                    act_all[partner, h], down_w[depth, source], preferred_element_type=f32
                )
                if place:
                    product = product + down_own[side, :, target]
                if last and side == 0:
                    pair_out[:, target] = product.astype(bf16)
                else:
                    down_own[side, :, target] = product
                return carry

            lax.fori_loop(0, width // TILE, down_columns, 0)
            if last and side == 0:
                pair_copy = send(pair_out, pair_in, pair_send, pair_recv, in_pair)
    pair_copy.wait_recv()
    expert_out[...] = (
        (down_own[1] + pair_in[...].astype(f32)).astype(bf16).reshape(n_dp, cap, width)
    )
    back_copies = [
        send(
            expert_out.at[flip(dp, i)],
            returned.at[dp],
            back_send.at[i],
            back_recv.at[i],
            in_line(i),
        )
        for i in range(n_dp - 1, 0, -1)
    ]
    returned[dp] = expert_out[dp]

    for copy in stat_copies:
        copy.wait_recv()
    stats = stat_in[0]
    for j in range(1, group):
        stats = stats + stat_in[j]
    token_scale = lax.rsqrt(stats[1, 0:1, 0:tokens] / features + norm_epsilon)
    logits = stats[0, :, 0:tokens] * token_scale
    chosen = [jnp.sum(logits * onehot[k], axis=0, keepdims=True) for k in range(2)]
    weights = jnp.zeros((slots, tokens), f32)
    for k in range(2):
        mixing = 1.0 / (1.0 + jnp.exp(chosen[1 - k] - chosen[k]))
        weights = weights + hit[k] * mixing
    high = weights.astype(bf16)
    low = (weights - high.astype(f32)).astype(bf16)
    for copy in back_copies:
        copy.wait_recv()
    back = returned[...].reshape(slots, width)
    tn = (((0,), (0,)), ((), ()))
    combined = lax.dot_general(high, back, tn, preferred_element_type=f32) + lax.dot_general(
        low, back, tn, preferred_element_type=f32
    )
    out_ref[...] = (hidden[...].astype(f32) + combined).astype(out_ref.dtype)

    for copies in (att_copies, row_copies, pre_copies, act_copies):
        for copy in copies.values():
            copy.wait_send()
    for copy in stat_copies + square_copies + back_copies + [pair_copy]:
        copy.wait_send()


def fused_layer(
    queries,
    key_cache,
    cached_values,
    incoming_keys,
    incoming_values,
    lengths,
    residual,
    out_proj,
    norm_gain,
    router,
    gate_proj,
    up_proj,
    down_proj,
    routes,
):
    n_sect, n_dp, n_tp = (lax.axis_size(name) for name in ("sect", "dp", "tp"))
    group = n_sect * n_tp
    tokens, width = residual.shape
    experts = router.shape[1]
    cap = tokens // 2
    slots = experts * cap
    rows = n_dp * cap
    share = gate_proj.shape[1] // n_sect
    f32, bf16 = jnp.float32, jnp.bfloat16
    vmem = pl.BlockSpec(memory_space=pltpu.VMEM)
    hbm = pl.BlockSpec(memory_space=pl.ANY)
    dma = pltpu.SemaphoreType.DMA
    seq, heads, head_size = queries.shape
    buffers = [
        (key_cache.shape, bf16),
        (cached_values.shape, bf16),
        (queries.shape, f32),
        ((heads, seq, head_size), bf16),
        (out_proj.shape, bf16),
        (gate_proj.shape, bf16),
        (up_proj.shape, bf16),
        (down_proj.shape, bf16),
        ((n_tp, heads, tokens, head_size), bf16),
        ((tokens, width), bf16),
        ((2, slots, tokens), f32),
        ((experts, cap, width), bf16),
        ((n_tp, rows, width), bf16),
        ((rows, n_tp * width), bf16),
        ((rows, 128), f32),
        ((n_sect, rows, 128), f32),
        ((3, 2, 2, rows, share // 2), bf16),
        ((3, 2, 2, rows, share // 2), bf16),
        ((2, 2, rows, share // 2), f32),
        ((n_sect, 2, rows, share // 2), bf16),
        ((2, rows, width), f32),
        ((rows, width), bf16),
        ((rows, width), bf16),
        ((n_dp, cap, width), bf16),
        ((experts, cap, width), bf16),
        ((2, 8, 128), f32),
        ((group, 2, 8, 128), f32),
    ]
    semaphores = [dma((2, 4)), dma((4,))]
    for count in (2 * n_sect, 2 * n_dp, group, n_sect, 6, 2 * n_sect):
        semaphores += [dma((count,)), dma((count,))]
    semaphores += [dma, dma, dma((n_dp,)), dma((n_dp,))]
    return pl.pallas_call(
        functools.partial(layer_kernel, (n_sect, n_dp, n_tp)),
        out_shape=jax.ShapeDtypeStruct((tokens, width), bf16),
        in_specs=[vmem] * 3
        + [pl.BlockSpec(memory_space=pltpu.SMEM)]
        + [vmem] * 4
        + [hbm] * 6,
        out_specs=vmem,
        scratch_shapes=[pltpu.VMEM(shape, kind) for shape, kind in buffers] + semaphores,
        compiler_params=pltpu.CompilerParams(
            collective_id=0, has_side_effects=True, vmem_limit_bytes=62 * 1024 * 1024
        ),
    )(
        queries,
        incoming_keys,
        incoming_values,
        lengths,
        residual,
        norm_gain.reshape(group, 1, width),
        router.T,
        routes.T,
        key_cache,
        cached_values,
        out_proj,
        gate_proj,
        up_proj,
        down_proj,
    )


def per_device(
    queries,
    key_cache,
    cached_values,
    incoming_keys,
    incoming_values,
    lengths,
    residual,
    out_proj,
    norm_gain,
    router,
    gate_proj,
    up_proj,
    down_proj,
    routes,
):
    fits = lax.axis_size("sect") == 4 and lax.axis_size("tp") == 2
    if fits and residual.shape[1] % TILE == 0:
        return fused_layer(
            queries[0],
            key_cache[0],
            cached_values[0],
            incoming_keys[0],
            incoming_values[0],
            lengths,
            residual,
            out_proj,
            norm_gain,
            router,
            gate_proj[0],
            up_proj[0],
            down_proj[0],
            routes,
        )
    attended = attend(
        queries[0], key_cache[0], cached_values[0], incoming_keys[0], incoming_values[0], lengths[0]
    )
    seq_local = attended.shape[0]
    tp_count = lax.axis_size("tp")
    head_width = attended.shape[1]
    column_count = out_proj.shape[1]
    weight_split = out_proj.reshape(tp_count, head_width, column_count)
    initial = jnp.zeros((residual.shape[0], column_count), jnp.float32)
    shards = lax.all_gather(attended[None], ("sect", "tp"), axis=0, tiled=True)

    def add_one(counter, current):
        head_block = lax.dynamic_index_in_dim(shards, counter, 0, keepdims=False)
        weight = lax.dynamic_index_in_dim(weight_split, counter % tp_count, 0, keepdims=False)
        product = jnp.dot(head_block, weight, preferred_element_type=jnp.float32)
        row_start = counter // tp_count * seq_local
        earlier = lax.dynamic_slice_in_dim(current, row_start, seq_local, 0)
        return lax.dynamic_update_slice_in_dim(current, earlier + product, row_start, 0)

    projected = lax.fori_loop(0, shards.shape[0], add_one, initial)
    hidden = (residual.astype(jnp.float32) + projected).astype(jnp.bfloat16)
    group_rows = residual.shape[0]
    capacity = group_rows // 2
    expert_count = router.shape[1]
    slot_total = expert_count * capacity
    flat_routes = routes.reshape(-1)
    onehot = (flat_routes[:, None] == jnp.arange(expert_count, dtype=jnp.int32)[None, :]).astype(
        jnp.int32
    )
    earlier_count = jnp.cumsum(onehot, axis=0) - onehot
    target = flat_routes * capacity + jnp.sum(earlier_count * onehot, axis=1)
    matches = target[None, :] == jnp.arange(slot_total, dtype=jnp.int32)[:, None]
    route_token = jnp.arange(flat_routes.shape[0], dtype=jnp.int32) // 2
    slot_token = jnp.sum(jnp.where(matches, route_token[None, :], 0), axis=1)
    slot_used = jnp.any(matches, axis=1)
    full_width = lax.all_gather(hidden, ("sect", "tp"), axis=1, tiled=True)
    normed = normalize(full_width, norm_gain)
    logits = jnp.dot(normed, router, preferred_element_type=jnp.float32)
    chosen = jnp.take_along_axis(logits, routes, axis=1)
    mixing = jax.nn.sigmoid(chosen - chosen[:, ::-1])
    own_share = width_share(normed)
    taken = jnp.take(own_share, slot_token, axis=0)
    outgoing = jnp.where(slot_used[:, None], taken, jnp.zeros((), own_share.dtype)).reshape(
        expert_count, 1, capacity, own_share.shape[1]
    )
    returned = lax.all_to_all(
        expert_ffn(
            lax.all_to_all(outgoing, "dp", split_axis=0, concat_axis=1, tiled=True),
            gate_proj,
            up_proj,
            down_proj,
        ),
        "dp",
        split_axis=1,
        concat_axis=0,
        tiled=True,
    )
    mix_flat = mixing.reshape(-1)
    returned_rows = returned.reshape(slot_total, -1)[target].astype(jnp.float32)
    combined = jnp.sum(
        mix_flat.reshape(group_rows, 2)[:, :, None] * returned_rows.reshape(group_rows, 2, -1),
        axis=1,
    )
    return (hidden.astype(jnp.float32) + combined).astype(jnp.bfloat16)


def solution(mesh):
    placed = (
        P("dp", "sect", "tp", None),
        P("dp", "sect", "tp", None, None),
        P("dp", "sect", "tp", None, None),
        P("dp", "sect", "tp", None),
        P("dp", "sect", "tp", None),
        P("dp", "sect"),
        P("dp", ("sect", "tp")),
        P(None, ("sect", "tp")),
        P(),
        P(),
        P("dp", "sect", "tp"),
        P("dp", "sect", "tp"),
        P("dp", "tp", "sect"),
        P("dp", None),
    )
    return jax.shard_map(
        per_device, mesh=mesh, in_specs=placed, out_specs=P("dp", ("sect", "tp")), check_vma=False
    )
```

```python
import functools
import math

import jax
import jax.numpy as jnp
from jax import lax
from jax.experimental import pallas as pl
from jax.experimental.pallas import tpu as pltpu
from jax.sharding import PartitionSpec as P

norm_epsilon = 1e-05
MESH = pl.DeviceIdType.MESH
TILE = 256


def attend(queries, key_cache, cached_values, incoming_keys, incoming_values, lengths):
    tokens = queries.shape[0]
    query_heads = queries.shape[1]
    head_size = queries.shape[2]
    kv_heads = key_cache.shape[1]
    heads_per_group = query_heads // kv_heads
    logit_scale = 1.0 / math.sqrt(head_size)
    query_head_groups = queries.reshape(tokens, kv_heads, heads_per_group, head_size)
    cached_entries = (
        jnp.einsum(
            "bkgd,bkpd->bkgp", query_head_groups, key_cache, preferred_element_type=jnp.float32
        )
        * logit_scale
    )
    new_token_score = (
        jnp.einsum(
            "ncwt,nct->ncw", query_head_groups, incoming_keys, preferred_element_type=jnp.float32
        )
        * logit_scale
    )
    positions = jnp.arange(key_cache.shape[2], dtype=jnp.int32)
    valid_slots = positions[None, :] < lengths[:, None]
    cached_entries = jnp.where(valid_slots[:, None, None, :], cached_entries, -jnp.inf)
    highest = jnp.maximum(jnp.max(cached_entries, axis=-1), new_token_score)
    cached_exp = jnp.exp(cached_entries - highest[..., None])
    fresh_exp = jnp.exp(new_token_score - highest)
    denominator = jnp.sum(cached_exp, axis=-1) + fresh_exp
    cached_prob = (cached_exp / denominator[..., None]).astype(jnp.bfloat16)
    fresh_prob = (fresh_exp / denominator).astype(jnp.bfloat16)
    gathered = jnp.einsum(
        "bkgp,bkpd->bkgd", cached_prob, cached_values, preferred_element_type=jnp.float32
    )
    gathered = (
        gathered
        + fresh_prob.astype(jnp.float32)[..., None]
        * incoming_values.astype(jnp.float32)[:, :, None, :]
    )
    return gathered.reshape(tokens, query_heads * head_size).astype(jnp.bfloat16)


def normalize(rows_in, norm_gain):
    values = rows_in.astype(jnp.float32)
    mean_square = jnp.mean(values * values, axis=-1, keepdims=True)
    return (values * lax.rsqrt(mean_square + norm_epsilon) * norm_gain).astype(jnp.bfloat16)


def width_share(rows_in):
    share = rows_in.shape[-1] // lax.axis_size("sect")
    return lax.dynamic_slice_in_dim(
        rows_in, lax.axis_index("sect") * share, share, rows_in.ndim - 1
    )


def expert_ffn(arrived, gate_proj, up_proj, down_proj):
    gate_pre = jnp.einsum("esnd,edf->esnf", arrived, gate_proj, preferred_element_type=jnp.float32)
    up_pre = jnp.einsum("esnd,edf->esnf", arrived, up_proj, preferred_element_type=jnp.float32)
    pre = jnp.stack([gate_pre, up_pre]).astype(jnp.bfloat16)
    total = lax.psum_scatter(pre, "sect", scatter_dimension=4, tiled=True).astype(jnp.float32)
    share = (jax.nn.silu(total[0]) * total[1]).astype(jnp.bfloat16)
    activated = lax.all_gather(share, "sect", axis=3, tiled=True)
    partial_out = jnp.einsum(
        "esnf,efd->esnd", activated, down_proj, preferred_element_type=jnp.float32
    )
    return lax.psum_scatter(partial_out.astype(jnp.bfloat16), "tp", scatter_dimension=3, tiled=True)


def layer_kernel(
    sizes,
    queries_ref,
    fresh_keys_ref,
    fresh_values_ref,
    lengths_ref,
    residual_ref,
    gain_ref,
    router_ref,
    routes_ref,
    keys_hbm,
    values_hbm,
    out_proj_hbm,
    gate_hbm,
    up_hbm,
    down_hbm,
    out_ref,
    keys,
    values,
    by_token,
    attended,
    out_w,
    gate_w,
    up_w,
    down_w,
    att_all,
    hidden,
    hit,
    outgoing,
    arrived,
    expert_in,
    square_out,
    square_in,
    pre_out,
    pre_in,
    pre_own,
    act_all,
    down_own,
    pair_out,
    pair_in,
    expert_out,
    returned,
    stat_out,
    stat_in,
    cache_sem,
    weight_sem,
    att_send,
    att_recv,
    row_send,
    row_recv,
    stat_send,
    stat_recv,
    square_send,
    square_recv,
    pre_send,
    pre_recv,
    act_send,
    act_recv,
    pair_send,
    pair_recv,
    back_send,
    back_recv,
):
    n_sect, n_dp, n_tp = sizes
    sect = lax.axis_index("sect")
    dp = lax.axis_index("dp")
    tp = lax.axis_index("tp")
    group = n_sect * n_tp
    me = sect * n_tp + tp
    f32, bf16 = jnp.float32, jnp.bfloat16

    def flip(value, bits):
        result = value
        bit = 1
        while bit <= bits:
            if bits & bit:
                result = result + bit - 2 * bit * ((value // bit) % 2)
            bit *= 2
        return result

    def in_group(j):
        other = flip(me, j)
        return {"sect": other // n_tp, "dp": dp, "tp": other % n_tp}

    def in_sect(j):
        return {"sect": flip(sect, j), "dp": dp, "tp": tp}

    def in_line(i):
        return {"sect": sect, "dp": flip(dp, i), "tp": tp}

    pair = flip(tp, 1)
    in_pair = {"sect": sect, "dp": dp, "tp": pair}

    def send(source, target, send_sem, recv_sem, device):
        copy = pltpu.make_async_remote_copy(
            src_ref=source,
            dst_ref=target,
            send_sem=send_sem,
            recv_sem=recv_sem,
            device_id=device,
            device_id_type=MESH,
        )
        copy.start()
        return copy

    seq, query_heads, head_size = queries_ref.shape
    pieces = 4
    cache_loads = []
    for piece in range(pieces):
        span = pl.ds(piece * (seq // pieces), seq // pieces)
        for which, (source, target) in enumerate(((keys_hbm, keys), (values_hbm, values))):
            copy = pltpu.make_async_copy(
                source.at[span], target.at[span], cache_sem.at[which, piece]
            )
            copy.start()
            cache_loads.append(copy)
    weights = ((out_proj_hbm, out_w), (gate_hbm, gate_w), (up_hbm, up_w), (down_hbm, down_w))

    def load(index):
        source, target = weights[index]
        depth = source.shape[0] // 4
        for part in range(4):
            pltpu.make_async_copy(
                source.at[pl.ds(part * depth, depth)],
                target.at[pl.ds(part * depth, depth)],
                weight_sem.at[index],
            ).start()

    def loaded(index):
        source, target = weights[index]
        pltpu.make_async_copy(source, target, weight_sem.at[index]).wait()

    barrier = pltpu.get_barrier_semaphore()
    for j in range(1, group):
        pl.semaphore_signal(barrier, inc=1, device_id=in_group(j), device_id_type=MESH)
    for i in range(1, n_dp):
        pl.semaphore_signal(barrier, inc=1, device_id=in_line(i), device_id_type=MESH)

    kv_heads, context = keys.shape[1], keys.shape[2]
    per_group = query_heads // kv_heads
    every = kv_heads * context
    nt = (((1,), (1,)), ((), ()))
    head_of_row = lax.broadcasted_iota(jnp.int32, (query_heads, every), 0) // per_group
    slot_of_column = lax.broadcasted_iota(jnp.int32, (query_heads, every), 1)
    head_of_column = slot_of_column // context
    position = jnp.where(
        head_of_row == head_of_column, slot_of_column - head_of_column * context, context
    )
    fresh_same = (
        lax.broadcasted_iota(jnp.int32, (query_heads, kv_heads), 0) // per_group
    ) == lax.broadcasted_iota(jnp.int32, (query_heads, kv_heads), 1)
    logit_scale = 1.0 / math.sqrt(head_size)

    step = seq // pieces

    def rows_of(array, place):
        return array[place * query_heads : (place + 1) * query_heads]

    for piece in range(pieces):
        cache_loads[2 * piece].wait()
        cache_loads[2 * piece + 1].wait()
        if piece == pieces - 2:
            load(0)
        batch = range(piece * step, (piece + 1) * step)
        scores, fresh = [], []
        for b in batch:
            query = queries_ref[b]
            score = lax.dot_general(
                query, keys[b].reshape(every, head_size), nt, preferred_element_type=f32
            )
            scores.append(jnp.where(position < lengths_ref[0, b], score * logit_scale, -jnp.inf))
            score = lax.dot_general(query, fresh_keys_ref[b], nt, preferred_element_type=f32)
            fresh.append(jnp.where(fresh_same, score * logit_scale, -jnp.inf))
        scores = jnp.concatenate(scores, axis=0)
        fresh = jnp.concatenate(fresh, axis=0)
        highest = jnp.maximum(
            jnp.max(scores, axis=1, keepdims=True), jnp.max(fresh, axis=1, keepdims=True)
        )
        scores = jnp.exp(scores - highest)
        fresh = jnp.exp(fresh - highest)
        total = jnp.sum(scores, axis=1, keepdims=True) + jnp.sum(fresh, axis=1, keepdims=True)
        inverse = 1.0 / total
        scores = scores * inverse
        fresh = fresh * inverse
        for place, b in enumerate(batch):
            by_token[b] = jnp.dot(
                rows_of(scores, place).astype(bf16),
                values[b].reshape(every, head_size),
                preferred_element_type=f32,
            ) + jnp.dot(
                rows_of(fresh, place).astype(bf16), fresh_values_ref[b], preferred_element_type=f32
            )

    count = seq * query_heads
    row = lax.broadcasted_iota(jnp.int32, (count, count), 0)
    column = lax.broadcasted_iota(jnp.int32, (count, count), 1)
    source = (row % seq) * query_heads + row // seq
    order = jnp.where(column == source, 1.0, 0.0).astype(bf16)
    rows_by_token = by_token[...].reshape(count, head_size).astype(bf16)
    attended[...] = (
        jnp.dot(order, rows_by_token, preferred_element_type=f32)
        .astype(bf16)
        .reshape(query_heads, seq, head_size)
    )
    pl.semaphore_wait(barrier, group - 1 + n_dp - 1)


    def seq_rows(j):
        return pl.ds(pl.multiple_of(flip(sect, j) * seq, seq), seq)

    att_copies = {}
    for j in range(n_sect - 1, -1, -1):
        att_copies[j, j == 0] = send(
            attended,
            att_all.at[tp, :, seq_rows(0)],
            att_send.at[2 * j + (j == 0)],
            att_recv.at[2 * j + (j == 0)],
            in_sect(j) if j else in_pair,
        )
    att_all[tp, :, seq_rows(0), :] = attended[...]

    load(1)

    experts = router_ref.shape[0]
    tokens = routes_ref.shape[1]
    cap = tokens // 2
    slots = experts * cap
    choice = [routes_ref[k : k + 1, :] for k in range(2)]
    expert_ids = lax.broadcasted_iota(jnp.int32, (8, tokens), 0)
    onehot = [jnp.where(expert_ids == choice[k], 1.0, 0.0).astype(f32) for k in range(2)]
    before = jnp.where(
        lax.broadcasted_iota(jnp.int32, (tokens, tokens), 0)
        < lax.broadcasted_iota(jnp.int32, (tokens, tokens), 1),
        1.0,
        0.0,
    ).astype(bf16)
    rank = jnp.dot((onehot[0] + onehot[1]).astype(bf16), before, preferred_element_type=f32)
    slot_ids = lax.broadcasted_iota(jnp.int32, (slots, tokens), 0)
    for k in range(2):
        slot = jnp.sum(rank * onehot[k], axis=0, keepdims=True).astype(jnp.int32)
        hit[k] = jnp.where(slot_ids == choice[k] * cap + slot, 1.0, 0.0).astype(f32)

    for j in range(1, n_sect):
        att_copies[j, False].wait_recv()
        block = att_all.at[tp, :, seq_rows(j)]
        att_copies[j, True] = send(
            block, block, att_send.at[2 * j + 1], att_recv.at[2 * j + 1], in_pair
        )
    loaded(0)
    load(2)
    for j in range(n_sect):
        att_copies[j, True].wait_recv()

    half = query_heads * head_size
    width = out_w.shape[1]

    def project(n, carry):
        columns = pl.ds(pl.multiple_of(n * TILE, TILE), TILE)
        total = residual_ref[:, columns].astype(f32)
        for t in range(n_tp):
            heads = jnp.concatenate([att_all[t, head] for head in range(query_heads)], axis=1)
            total = total + jnp.dot(
                heads, out_w[t * half : (t + 1) * half, columns], preferred_element_type=f32
            )
        hidden[:, columns] = total.astype(bf16)
        return carry

    lax.fori_loop(0, width // TILE, project, 0)

    rows = jnp.dot((hit[0] + hit[1]).astype(bf16), hidden[...], preferred_element_type=f32)
    outgoing[...] = rows.astype(bf16).reshape(experts, cap, width)

    def line_rows(i):
        return pl.ds(pl.multiple_of(flip(dp, i) * cap, cap), cap)

    row_copies = {}
    for i in range(n_dp - 1, -1, -1):
        row_copies[i, i == 0] = send(
            outgoing.at[flip(dp, i)],
            arrived.at[tp, line_rows(0)],
            row_send.at[2 * i + (i == 0)],
            row_recv.at[2 * i + (i == 0)],
            in_line(i) if i else in_pair,
        )
    arrived[tp, line_rows(0), :] = outgoing[dp]

    own = hidden[...].astype(f32)
    scaled = (own * gain_ref[me]).astype(bf16)
    nt = (((1,), (1,)), ((), ()))
    router_part = router_ref[:, pl.ds(pl.multiple_of(me * width, width), width)]
    logit_part = lax.dot_general(router_part, scaled, nt, preferred_element_type=f32)
    square = own * own
    square_high = square.astype(bf16)
    square_low = (square - square_high.astype(f32)).astype(bf16)
    ones = jnp.ones((8, width), bf16)
    square_part = lax.dot_general(
        ones, square_high, nt, preferred_element_type=f32
    ) + lax.dot_general(ones, square_low, nt, preferred_element_type=f32)
    stat_out[...] = jnp.zeros_like(stat_out)
    stat_out[0, 0:experts, 0:tokens] = logit_part
    stat_out[1, :, 0:tokens] = square_part
    stat_copies = []
    for j in range(1, group):
        copy = pltpu.make_async_remote_copy(
            src_ref=stat_out,
            dst_ref=stat_in.at[me],
            send_sem=stat_send.at[j],
            recv_sem=stat_recv.at[j],
            device_id=in_group(j),
            device_id_type=MESH,
        )
        copy.start()
        stat_copies.append(copy)
    stat_in[me] = stat_out[...]

    for i in range(1, n_dp):
        row_copies[i, False].wait_recv()
        block = arrived.at[tp, line_rows(i)]
        row_copies[i, True] = send(
            block, block, row_send.at[2 * i + 1], row_recv.at[2 * i + 1], in_pair
        )

    def take(t):
        part = arrived[t].astype(f32)
        columns = pl.ds(pl.multiple_of(t * width, width), width)
        expert_in[:, columns] = (part * gain_ref[sect * n_tp + t]).astype(bf16)
        return jnp.sum(part * part, axis=1, keepdims=True)

    total_square = take(tp)
    for i in range(n_dp):
        row_copies[i, True].wait_recv()
    total_square = total_square + take(pair)
    square_out[...] = jnp.broadcast_to(total_square, square_out.shape)
    square_copies = [
        send(square_out, square_in.at[j], square_send.at[j], square_recv.at[j], in_sect(j))
        for j in range(1, n_sect)
    ]

    loaded(1)
    loaded(2)
    load(3)
    share = gate_w.shape[1] // n_sect
    part_width = share // 2
    steps = part_width // TILE
    first, second = (1, 2), (2, 1)

    def products(j, h, store):
        start = flip(sect, j) * share + h * part_width

        def columns_of(n, carry):
            source = pl.ds(pl.multiple_of(start + n * TILE, TILE), TILE)
            target = pl.ds(pl.multiple_of(n * TILE, TILE), TILE)
            for which, weight in enumerate((gate_w, up_w)):
                product = jnp.dot(expert_in[...], weight[:, source], preferred_element_type=f32)
                store(which, target, product)
            return carry

        lax.fori_loop(0, steps, columns_of, 0)

    def pass_on(kind, h, j):
        index = 2 * kind + h
        return send(
            pre_out.at[kind, h],
            pre_in.at[kind, h],
            pre_send.at[index],
            pre_recv.at[index],
            in_sect(j),
        )

    pre_copies = {}
    for kind in range(2):
        for h in range(2):

            def store_out(which, target, product):
                pre_out[kind, h, which, :, target] = product.astype(bf16)

            products(3 if kind == 0 else first[h], h, store_out)
            pre_copies[kind, h] = pass_on(kind, h, first[h])
    for h in range(2):

        def store_pass(which, target, product):
            pre_own[h, which, :, target] = product

        products(second[h], h, store_pass)
    for h in range(2):
        pre_copies[0, h].wait_recv()

        def add_pass(n, carry):
            target = pl.ds(pl.multiple_of(n * TILE, TILE), TILE)
            for which in range(2):
                total = pre_own[h, which, :, target] + pre_in[0, h, which, :, target].astype(f32)
                pre_out[2, h, which, :, target] = total.astype(bf16)
            return carry

        lax.fori_loop(0, steps, add_pass, 0)
        pre_copies[2, h] = pass_on(2, h, second[h])
    for h in range(2):

        def store_own(which, target, product):
            pre_own[h, which, :, target] = product

        products(0, h, store_own)

    for copy in square_copies:
        copy.wait_recv()
    summed = square_out[:, 0:1]
    for j in range(1, n_sect):
        summed = summed + square_in[j, :, 0:1]
    features = n_sect * n_tp * width
    scale = lax.rsqrt(summed / features + norm_epsilon)
    act_copies = {}

    def share_act(j, h, block, to):
        index = 2 * j + h
        act_copies[j, h] = send(
            act_all.at[block, h],
            act_all.at[block, h],
            act_send.at[index],
            act_recv.at[index],
            in_sect(to),
        )

    for h in range(2):
        pre_copies[1, h].wait_recv()
        pre_copies[2, h].wait_recv()

        def activate(n, carry):
            target = pl.ds(pl.multiple_of(n * TILE, TILE), TILE)
            sums = []
            for which in range(2):
                total = pre_own[h, which, :, target] + pre_in[1, h, which, :, target].astype(f32)
                total = total + pre_in[2, h, which, :, target].astype(f32)
                sums.append(total * scale)
            active = sums[0] / (1.0 + jnp.exp(-sums[0])) * sums[1]
            act_all[sect, h, :, target] = active.astype(bf16)
            return carry

        lax.fori_loop(0, steps, activate, 0)
        share_act(first[h], h, sect, first[h])
    for h in range(2):
        share_act(second[h], h, sect, second[h])

    loaded(3)
    order = ((0, 0), (0, 1), (1, 0), (2, 1), (1, 1), (2, 0), (3, 0), (3, 1))
    for place, (j, h) in enumerate(order):
        partner = flip(sect, j)
        if j:
            act_copies[j, h].wait_recv()
        if (j, h) in ((1, 0), (2, 1)):
            share_act(3, h, partner, second[h])
        last = place == len(order) - 1
        depth = pl.ds(pl.multiple_of(partner * share + h * part_width, part_width), part_width)
        for side in range(2):
            owner = pair if side == 0 else tp

            def down_columns(n, carry):
                source = pl.ds(pl.multiple_of(owner * width + n * TILE, TILE), TILE)
                target = pl.ds(pl.multiple_of(n * TILE, TILE), TILE)
                product = jnp.dot(
                    act_all[partner, h], down_w[depth, source], preferred_element_type=f32
                )
                if place:
                    product = product + down_own[side, :, target]
                if last and side == 0:
                    pair_out[:, target] = product.astype(bf16)
                else:
                    down_own[side, :, target] = product
                return carry

            lax.fori_loop(0, width // TILE, down_columns, 0)
            if last and side == 0:
                pair_copy = send(pair_out, pair_in, pair_send, pair_recv, in_pair)
    pair_copy.wait_recv()
    expert_out[...] = (
        (down_own[1] + pair_in[...].astype(f32)).astype(bf16).reshape(n_dp, cap, width)
    )
    back_copies = [
        send(
            expert_out.at[flip(dp, i)],
            returned.at[dp],
            back_send.at[i],
            back_recv.at[i],
            in_line(i),
        )
        for i in range(n_dp - 1, 0, -1)
    ]
    returned[dp] = expert_out[dp]

    for copy in stat_copies:
        copy.wait_recv()
    stats = stat_in[0]
    for j in range(1, group):
        stats = stats + stat_in[j]
    token_scale = lax.rsqrt(stats[1, 0:1, 0:tokens] / features + norm_epsilon)
    logits = stats[0, :, 0:tokens] * token_scale
    chosen = [jnp.sum(logits * onehot[k], axis=0, keepdims=True) for k in range(2)]
    weights = jnp.zeros((slots, tokens), f32)
    for k in range(2):
        mixing = 1.0 / (1.0 + jnp.exp(chosen[1 - k] - chosen[k]))
        weights = weights + hit[k] * mixing
    high = weights.astype(bf16)
    low = (weights - high.astype(f32)).astype(bf16)
    for copy in back_copies:
        copy.wait_recv()
    back = returned[...].reshape(slots, width)
    tn = (((0,), (0,)), ((), ()))
    combined = lax.dot_general(high, back, tn, preferred_element_type=f32) + lax.dot_general(
        low, back, tn, preferred_element_type=f32
    )
    out_ref[...] = (hidden[...].astype(f32) + combined).astype(out_ref.dtype)

    for copies in (att_copies, row_copies, pre_copies, act_copies):
        for copy in copies.values():
            copy.wait_send()
    for copy in stat_copies + square_copies + back_copies + [pair_copy]:
        copy.wait_send()


def fused_layer(
    queries,
    key_cache,
    cached_values,
    incoming_keys,
    incoming_values,
    lengths,
    residual,
    out_proj,
    norm_gain,
    router,
    gate_proj,
    up_proj,
    down_proj,
    routes,
):
    n_sect, n_dp, n_tp = (lax.axis_size(name) for name in ("sect", "dp", "tp"))
    group = n_sect * n_tp
    tokens, width = residual.shape
    experts = router.shape[1]
    cap = tokens // 2
    slots = experts * cap
    rows = n_dp * cap
    share = gate_proj.shape[1] // n_sect
    f32, bf16 = jnp.float32, jnp.bfloat16
    vmem = pl.BlockSpec(memory_space=pltpu.VMEM)
    hbm = pl.BlockSpec(memory_space=pl.ANY)
    dma = pltpu.SemaphoreType.DMA
    seq, heads, head_size = queries.shape
    buffers = [
        (key_cache.shape, bf16),
        (cached_values.shape, bf16),
        (queries.shape, f32),
        ((heads, seq, head_size), bf16),
        (out_proj.shape, bf16),
        (gate_proj.shape, bf16),
        (up_proj.shape, bf16),
        (down_proj.shape, bf16),
        ((n_tp, heads, tokens, head_size), bf16),
        ((tokens, width), bf16),
        ((2, slots, tokens), f32),
        ((experts, cap, width), bf16),
        ((n_tp, rows, width), bf16),
        ((rows, n_tp * width), bf16),
        ((rows, 128), f32),
        ((n_sect, rows, 128), f32),
        ((3, 2, 2, rows, share // 2), bf16),
        ((3, 2, 2, rows, share // 2), bf16),
        ((2, 2, rows, share // 2), f32),
        ((n_sect, 2, rows, share // 2), bf16),
        ((2, rows, width), f32),
        ((rows, width), bf16),
        ((rows, width), bf16),
        ((n_dp, cap, width), bf16),
        ((experts, cap, width), bf16),
        ((2, 8, 128), f32),
        ((group, 2, 8, 128), f32),
    ]
    semaphores = [dma((2, 4)), dma((4,))]
    for count in (2 * n_sect, 2 * n_dp, group, n_sect, 6, 2 * n_sect):
        semaphores += [dma((count,)), dma((count,))]
    semaphores += [dma, dma, dma((n_dp,)), dma((n_dp,))]
    return pl.pallas_call(
        functools.partial(layer_kernel, (n_sect, n_dp, n_tp)),
        out_shape=jax.ShapeDtypeStruct((tokens, width), bf16),
        in_specs=[vmem] * 3
        + [pl.BlockSpec(memory_space=pltpu.SMEM)]
        + [vmem] * 4
        + [hbm] * 6,
        out_specs=vmem,
        scratch_shapes=[pltpu.VMEM(shape, kind) for shape, kind in buffers] + semaphores,
        compiler_params=pltpu.CompilerParams(
            collective_id=0, has_side_effects=True, vmem_limit_bytes=62 * 1024 * 1024
        ),
    )(
        queries,
        incoming_keys,
        incoming_values,
        lengths,
        residual,
        norm_gain.reshape(group, 1, width),
        router.T,
        routes.T,
        key_cache,
        cached_values,
        out_proj,
        gate_proj,
        up_proj,
        down_proj,
    )


def per_device(
    queries,
    key_cache,
    cached_values,
    incoming_keys,
    incoming_values,
    lengths,
    residual,
    out_proj,
    norm_gain,
    router,
    gate_proj,
    up_proj,
    down_proj,
    routes,
):
    fits = lax.axis_size("sect") == 4 and lax.axis_size("tp") == 2
    if fits and residual.shape[1] % TILE == 0:
        return fused_layer(
            queries[0],
            key_cache[0],
            cached_values[0],
            incoming_keys[0],
            incoming_values[0],
            lengths,
            residual,
            out_proj,
            norm_gain,
            router,
            gate_proj[0],
            up_proj[0],
            down_proj[0],
            routes,
        )
    attended = attend(
        queries[0], key_cache[0], cached_values[0], incoming_keys[0], incoming_values[0], lengths[0]
    )
    seq_local = attended.shape[0]
    tp_count = lax.axis_size("tp")
    head_width = attended.shape[1]
    column_count = out_proj.shape[1]
    weight_split = out_proj.reshape(tp_count, head_width, column_count)
    initial = jnp.zeros((residual.shape[0], column_count), jnp.float32)
    shards = lax.all_gather(attended[None], ("sect", "tp"), axis=0, tiled=True)

    def add_one(counter, current):
        head_block = lax.dynamic_index_in_dim(shards, counter, 0, keepdims=False)
        weight = lax.dynamic_index_in_dim(weight_split, counter % tp_count, 0, keepdims=False)
        product = jnp.dot(head_block, weight, preferred_element_type=jnp.float32)
        row_start = counter // tp_count * seq_local
        earlier = lax.dynamic_slice_in_dim(current, row_start, seq_local, 0)
        return lax.dynamic_update_slice_in_dim(current, earlier + product, row_start, 0)

    projected = lax.fori_loop(0, shards.shape[0], add_one, initial)
    hidden = (residual.astype(jnp.float32) + projected).astype(jnp.bfloat16)
    group_rows = residual.shape[0]
    capacity = group_rows // 2
    expert_count = router.shape[1]
    slot_total = expert_count * capacity
    flat_routes = routes.reshape(-1)
    onehot = (flat_routes[:, None] == jnp.arange(expert_count, dtype=jnp.int32)[None, :]).astype(
        jnp.int32
    )
    earlier_count = jnp.cumsum(onehot, axis=0) - onehot
    target = flat_routes * capacity + jnp.sum(earlier_count * onehot, axis=1)
    matches = target[None, :] == jnp.arange(slot_total, dtype=jnp.int32)[:, None]
    route_token = jnp.arange(flat_routes.shape[0], dtype=jnp.int32) // 2
    slot_token = jnp.sum(jnp.where(matches, route_token[None, :], 0), axis=1)
    slot_used = jnp.any(matches, axis=1)
    full_width = lax.all_gather(hidden, ("sect", "tp"), axis=1, tiled=True)
    normed = normalize(full_width, norm_gain)
    logits = jnp.dot(normed, router, preferred_element_type=jnp.float32)
    chosen = jnp.take_along_axis(logits, routes, axis=1)
    mixing = jax.nn.sigmoid(chosen - chosen[:, ::-1])
    own_share = width_share(normed)
    taken = jnp.take(own_share, slot_token, axis=0)
    outgoing = jnp.where(slot_used[:, None], taken, jnp.zeros((), own_share.dtype)).reshape(
        expert_count, 1, capacity, own_share.shape[1]
    )
    returned = lax.all_to_all(
        expert_ffn(
            lax.all_to_all(outgoing, "dp", split_axis=0, concat_axis=1, tiled=True),
            gate_proj,
            up_proj,
            down_proj,
        ),
        "dp",
        split_axis=1,
        concat_axis=0,
        tiled=True,
    )
    mix_flat = mixing.reshape(-1)
    returned_rows = returned.reshape(slot_total, -1)[target].astype(jnp.float32)
    combined = jnp.sum(
        mix_flat.reshape(group_rows, 2)[:, :, None] * returned_rows.reshape(group_rows, 2, -1),
        axis=1,
    )
    return (hidden.astype(jnp.float32) + combined).astype(jnp.bfloat16)


def solution(mesh):
    placed = (
        P("dp", "sect", "tp", None),
        P("dp", "sect", "tp", None, None),
        P("dp", "sect", "tp", None, None),
        P("dp", "sect", "tp", None),
        P("dp", "sect", "tp", None),
        P("dp", "sect"),
        P("dp", ("sect", "tp")),
        P(None, ("sect", "tp")),
        P(),
        P(),
        P("dp", "sect", "tp"),
        P("dp", "sect", "tp"),
        P("dp", "tp", "sect"),
        P("dp", None),
    )
    return jax.shard_map(
        per_device, mesh=mesh, in_specs=placed, out_specs=P("dp", ("sect", "tp")), check_vma=False
    )
```

```python
import functools
import math

import jax
import jax.numpy as jnp
from jax import lax
from jax.experimental import pallas as pl
from jax.experimental.pallas import tpu as pltpu
from jax.sharding import PartitionSpec as P

norm_epsilon = 1e-05
MESH = pl.DeviceIdType.MESH
TILE = 256


def attend(queries, key_cache, cached_values, incoming_keys, incoming_values, lengths):
    tokens = queries.shape[0]
    query_heads = queries.shape[1]
    head_size = queries.shape[2]
    kv_heads = key_cache.shape[1]
    heads_per_group = query_heads // kv_heads
    logit_scale = 1.0 / math.sqrt(head_size)
    query_head_groups = queries.reshape(tokens, kv_heads, heads_per_group, head_size)
    cached_entries = (
        jnp.einsum(
            "bkgd,bkpd->bkgp", query_head_groups, key_cache, preferred_element_type=jnp.float32
        )
        * logit_scale
    )
    new_token_score = (
        jnp.einsum(
            "ncwt,nct->ncw", query_head_groups, incoming_keys, preferred_element_type=jnp.float32
        )
        * logit_scale
    )
    positions = jnp.arange(key_cache.shape[2], dtype=jnp.int32)
    valid_slots = positions[None, :] < lengths[:, None]
    cached_entries = jnp.where(valid_slots[:, None, None, :], cached_entries, -jnp.inf)
    highest = jnp.maximum(jnp.max(cached_entries, axis=-1), new_token_score)
    cached_exp = jnp.exp(cached_entries - highest[..., None])
    fresh_exp = jnp.exp(new_token_score - highest)
    denominator = jnp.sum(cached_exp, axis=-1) + fresh_exp
    cached_prob = (cached_exp / denominator[..., None]).astype(jnp.bfloat16)
    fresh_prob = (fresh_exp / denominator).astype(jnp.bfloat16)
    gathered = jnp.einsum(
        "bkgp,bkpd->bkgd", cached_prob, cached_values, preferred_element_type=jnp.float32
    )
    gathered = (
        gathered
        + fresh_prob.astype(jnp.float32)[..., None]
        * incoming_values.astype(jnp.float32)[:, :, None, :]
    )
    return gathered.reshape(tokens, query_heads * head_size).astype(jnp.bfloat16)


def normalize(rows_in, norm_gain):
    values = rows_in.astype(jnp.float32)
    mean_square = jnp.mean(values * values, axis=-1, keepdims=True)
    return (values * lax.rsqrt(mean_square + norm_epsilon) * norm_gain).astype(jnp.bfloat16)


def width_share(rows_in):
    share = rows_in.shape[-1] // lax.axis_size("sect")
    return lax.dynamic_slice_in_dim(
        rows_in, lax.axis_index("sect") * share, share, rows_in.ndim - 1
    )


def expert_ffn(arrived, gate_proj, up_proj, down_proj):
    gate_pre = jnp.einsum("esnd,edf->esnf", arrived, gate_proj, preferred_element_type=jnp.float32)
    up_pre = jnp.einsum("esnd,edf->esnf", arrived, up_proj, preferred_element_type=jnp.float32)
    pre = jnp.stack([gate_pre, up_pre]).astype(jnp.bfloat16)
    total = lax.psum_scatter(pre, "sect", scatter_dimension=4, tiled=True).astype(jnp.float32)
    share = (jax.nn.silu(total[0]) * total[1]).astype(jnp.bfloat16)
    activated = lax.all_gather(share, "sect", axis=3, tiled=True)
    partial_out = jnp.einsum(
        "esnf,efd->esnd", activated, down_proj, preferred_element_type=jnp.float32
    )
    return lax.psum_scatter(partial_out.astype(jnp.bfloat16), "tp", scatter_dimension=3, tiled=True)


def layer_kernel(
    sizes,
    queries_ref,
    fresh_keys_ref,
    fresh_values_ref,
    lengths_ref,
    residual_ref,
    gain_ref,
    router_ref,
    routes_ref,
    keys_hbm,
    values_hbm,
    out_proj_hbm,
    gate_hbm,
    up_hbm,
    down_hbm,
    out_ref,
    keys,
    values,
    by_token,
    attended,
    out_w,
    gate_w,
    up_w,
    down_w,
    att_all,
    hidden,
    hit,
    outgoing,
    arrived,
    expert_in,
    square_out,
    square_in,
    pre_out,
    pre_in,
    pre_own,
    act_all,
    down_own,
    pair_out,
    pair_in,
    expert_out,
    returned,
    stat_out,
    stat_in,
    cache_sem,
    weight_sem,
    att_send,
    att_recv,
    row_send,
    row_recv,
    stat_send,
    stat_recv,
    square_send,
    square_recv,
    pre_send,
    pre_recv,
    act_send,
    act_recv,
    pair_send,
    pair_recv,
    back_send,
    back_recv,
):
    n_sect, n_dp, n_tp = sizes
    sect = lax.axis_index("sect")
    dp = lax.axis_index("dp")
    tp = lax.axis_index("tp")
    group = n_sect * n_tp
    me = sect * n_tp + tp
    f32, bf16 = jnp.float32, jnp.bfloat16

    def flip(value, bits):
        result = value
        bit = 1
        while bit <= bits:
            if bits & bit:
                result = result + bit - 2 * bit * ((value // bit) % 2)
            bit *= 2
        return result

    def in_group(j):
        other = flip(me, j)
        return {"sect": other // n_tp, "dp": dp, "tp": other % n_tp}

    def in_sect(j):
        return {"sect": flip(sect, j), "dp": dp, "tp": tp}

    def in_line(i):
        return {"sect": sect, "dp": flip(dp, i), "tp": tp}

    pair = flip(tp, 1)
    in_pair = {"sect": sect, "dp": dp, "tp": pair}

    def send(source, target, send_sem, recv_sem, device):
        copy = pltpu.make_async_remote_copy(
            src_ref=source,
            dst_ref=target,
            send_sem=send_sem,
            recv_sem=recv_sem,
            device_id=device,
            device_id_type=MESH,
        )
        copy.start()
        return copy

    seq, query_heads, head_size = queries_ref.shape
    pieces = 4
    cache_loads = []
    for piece in range(pieces):
        span = pl.ds(piece * (seq // pieces), seq // pieces)
        for which, (source, target) in enumerate(((keys_hbm, keys), (values_hbm, values))):
            copy = pltpu.make_async_copy(
                source.at[span], target.at[span], cache_sem.at[which, piece]
            )
            if piece < 2:
                copy.start()
            cache_loads.append(copy)
    weights = ((out_proj_hbm, out_w), (gate_hbm, gate_w), (up_hbm, up_w), (down_hbm, down_w))

    def load(index):
        source, target = weights[index]
        depth = source.shape[0] // 4
        for part in range(4):
            pltpu.make_async_copy(
                source.at[pl.ds(part * depth, depth)],
                target.at[pl.ds(part * depth, depth)],
                weight_sem.at[index],
            ).start()

    def loaded(index):
        source, target = weights[index]
        pltpu.make_async_copy(source, target, weight_sem.at[index]).wait()

    barrier = pltpu.get_barrier_semaphore()
    for j in range(1, group):
        pl.semaphore_signal(barrier, inc=1, device_id=in_group(j), device_id_type=MESH)
    for i in range(1, n_dp):
        pl.semaphore_signal(barrier, inc=1, device_id=in_line(i), device_id_type=MESH)

    kv_heads, context = keys.shape[1], keys.shape[2]
    per_group = query_heads // kv_heads
    every = kv_heads * context
    nt = (((1,), (1,)), ((), ()))
    head_of_row = lax.broadcasted_iota(jnp.int32, (query_heads, every), 0) // per_group
    slot_of_column = lax.broadcasted_iota(jnp.int32, (query_heads, every), 1)
    head_of_column = slot_of_column // context
    position = jnp.where(
        head_of_row == head_of_column, slot_of_column - head_of_column * context, context
    )
    fresh_same = (
        lax.broadcasted_iota(jnp.int32, (query_heads, kv_heads), 0) // per_group
    ) == lax.broadcasted_iota(jnp.int32, (query_heads, kv_heads), 1)
    logit_scale = 1.0 / math.sqrt(head_size)

    step = seq // pieces

    def rows_of(array, place):
        return array[place * query_heads : (place + 1) * query_heads]

    for piece in range(pieces):
        cache_loads[2 * piece].wait()
        cache_loads[2 * piece + 1].wait()
        if piece < pieces - 2:
            cache_loads[2 * piece + 4].start()
            cache_loads[2 * piece + 5].start()
        if piece == pieces - 2:
            load(0)
        batch = range(piece * step, (piece + 1) * step)
        scores, fresh = [], []
        for b in batch:
            query = queries_ref[b]
            score = lax.dot_general(
                query, keys[b].reshape(every, head_size), nt, preferred_element_type=f32
            )
            scores.append(jnp.where(position < lengths_ref[0, b], score * logit_scale, -jnp.inf))
            score = lax.dot_general(query, fresh_keys_ref[b], nt, preferred_element_type=f32)
            fresh.append(jnp.where(fresh_same, score * logit_scale, -jnp.inf))
        scores = jnp.concatenate(scores, axis=0)
        fresh = jnp.concatenate(fresh, axis=0)
        highest = jnp.maximum(
            jnp.max(scores, axis=1, keepdims=True), jnp.max(fresh, axis=1, keepdims=True)
        )
        scores = jnp.exp(scores - highest)
        fresh = jnp.exp(fresh - highest)
        total = jnp.sum(scores, axis=1, keepdims=True) + jnp.sum(fresh, axis=1, keepdims=True)
        inverse = 1.0 / total
        scores = scores * inverse
        fresh = fresh * inverse
        for place, b in enumerate(batch):
            by_token[b] = jnp.dot(
                rows_of(scores, place).astype(bf16),
                values[b].reshape(every, head_size),
                preferred_element_type=f32,
            ) + jnp.dot(
                rows_of(fresh, place).astype(bf16), fresh_values_ref[b], preferred_element_type=f32
            )

    count = seq * query_heads
    row = lax.broadcasted_iota(jnp.int32, (count, count), 0)
    column = lax.broadcasted_iota(jnp.int32, (count, count), 1)
    source = (row % seq) * query_heads + row // seq
    order = jnp.where(column == source, 1.0, 0.0).astype(bf16)
    rows_by_token = by_token[...].reshape(count, head_size).astype(bf16)
    attended[...] = (
        jnp.dot(order, rows_by_token, preferred_element_type=f32)
        .astype(bf16)
        .reshape(query_heads, seq, head_size)
    )
    pl.semaphore_wait(barrier, group - 1 + n_dp - 1)


    def seq_rows(j):
        return pl.ds(pl.multiple_of(flip(sect, j) * seq, seq), seq)

    att_copies = {}
    for j in range(n_sect - 1, -1, -1):
        att_copies[j, j == 0] = send(
            attended,
            att_all.at[tp, :, seq_rows(0)],
            att_send.at[2 * j + (j == 0)],
            att_recv.at[2 * j + (j == 0)],
            in_sect(j) if j else in_pair,
        )
    att_all[tp, :, seq_rows(0), :] = attended[...]

    load(1)

    experts = router_ref.shape[0]
    tokens = routes_ref.shape[1]
    cap = tokens // 2
    slots = experts * cap
    choice = [routes_ref[k : k + 1, :] for k in range(2)]
    expert_ids = lax.broadcasted_iota(jnp.int32, (8, tokens), 0)
    onehot = [jnp.where(expert_ids == choice[k], 1.0, 0.0).astype(f32) for k in range(2)]
    before = jnp.where(
        lax.broadcasted_iota(jnp.int32, (tokens, tokens), 0)
        < lax.broadcasted_iota(jnp.int32, (tokens, tokens), 1),
        1.0,
        0.0,
    ).astype(bf16)
    rank = jnp.dot((onehot[0] + onehot[1]).astype(bf16), before, preferred_element_type=f32)
    slot_ids = lax.broadcasted_iota(jnp.int32, (slots, tokens), 0)
    for k in range(2):
        slot = jnp.sum(rank * onehot[k], axis=0, keepdims=True).astype(jnp.int32)
        hit[k] = jnp.where(slot_ids == choice[k] * cap + slot, 1.0, 0.0).astype(f32)

    for j in range(1, n_sect):
        att_copies[j, False].wait_recv()
        block = att_all.at[tp, :, seq_rows(j)]
        att_copies[j, True] = send(
            block, block, att_send.at[2 * j + 1], att_recv.at[2 * j + 1], in_pair
        )
    loaded(0)
    load(2)
    for j in range(n_sect):
        att_copies[j, True].wait_recv()

    half = query_heads * head_size
    width = out_w.shape[1]

    def project(n, carry):
        columns = pl.ds(pl.multiple_of(n * TILE, TILE), TILE)
        total = residual_ref[:, columns].astype(f32)
        for t in range(n_tp):
            heads = jnp.concatenate([att_all[t, head] for head in range(query_heads)], axis=1)
            total = total + jnp.dot(
                heads, out_w[t * half : (t + 1) * half, columns], preferred_element_type=f32
            )
        hidden[:, columns] = total.astype(bf16)
        return carry

    lax.fori_loop(0, width // TILE, project, 0)

    rows = jnp.dot((hit[0] + hit[1]).astype(bf16), hidden[...], preferred_element_type=f32)
    outgoing[...] = rows.astype(bf16).reshape(experts, cap, width)

    def line_rows(i):
        return pl.ds(pl.multiple_of(flip(dp, i) * cap, cap), cap)

    row_copies = {}
    for i in range(n_dp - 1, -1, -1):
        row_copies[i, i == 0] = send(
            outgoing.at[flip(dp, i)],
            arrived.at[tp, line_rows(0)],
            row_send.at[2 * i + (i == 0)],
            row_recv.at[2 * i + (i == 0)],
            in_line(i) if i else in_pair,
        )
    arrived[tp, line_rows(0), :] = outgoing[dp]

    own = hidden[...].astype(f32)
    scaled = (own * gain_ref[me]).astype(bf16)
    nt = (((1,), (1,)), ((), ()))
    router_part = router_ref[:, pl.ds(pl.multiple_of(me * width, width), width)]
    logit_part = lax.dot_general(router_part, scaled, nt, preferred_element_type=f32)
    square = own * own
    square_high = square.astype(bf16)
    square_low = (square - square_high.astype(f32)).astype(bf16)
    ones = jnp.ones((8, width), bf16)
    square_part = lax.dot_general(
        ones, square_high, nt, preferred_element_type=f32
    ) + lax.dot_general(ones, square_low, nt, preferred_element_type=f32)
    stat_out[...] = jnp.zeros_like(stat_out)
    stat_out[0, 0:experts, 0:tokens] = logit_part
    stat_out[1, :, 0:tokens] = square_part
    stat_copies = []
    for j in range(1, group):
        copy = pltpu.make_async_remote_copy(
            src_ref=stat_out,
            dst_ref=stat_in.at[me],
            send_sem=stat_send.at[j],
            recv_sem=stat_recv.at[j],
            device_id=in_group(j),
            device_id_type=MESH,
        )
        copy.start()
        stat_copies.append(copy)
    stat_in[me] = stat_out[...]

    for i in range(1, n_dp):
        row_copies[i, False].wait_recv()
        block = arrived.at[tp, line_rows(i)]
        row_copies[i, True] = send(
            block, block, row_send.at[2 * i + 1], row_recv.at[2 * i + 1], in_pair
        )

    def take(t):
        part = arrived[t].astype(f32)
        columns = pl.ds(pl.multiple_of(t * width, width), width)
        expert_in[:, columns] = (part * gain_ref[sect * n_tp + t]).astype(bf16)
        return jnp.sum(part * part, axis=1, keepdims=True)

    total_square = take(tp)
    for i in range(n_dp):
        row_copies[i, True].wait_recv()
    total_square = total_square + take(pair)
    square_out[...] = jnp.broadcast_to(total_square, square_out.shape)
    square_copies = [
        send(square_out, square_in.at[j], square_send.at[j], square_recv.at[j], in_sect(j))
        for j in range(1, n_sect)
    ]

    loaded(1)
    loaded(2)
    load(3)
    share = gate_w.shape[1] // n_sect
    part_width = share // 2
    steps = part_width // TILE
    first, second = (1, 2), (2, 1)

    def products(j, h, store):
        start = flip(sect, j) * share + h * part_width

        def columns_of(n, carry):
            source = pl.ds(pl.multiple_of(start + n * TILE, TILE), TILE)
            target = pl.ds(pl.multiple_of(n * TILE, TILE), TILE)
            for which, weight in enumerate((gate_w, up_w)):
                product = jnp.dot(expert_in[...], weight[:, source], preferred_element_type=f32)
                store(which, target, product)
            return carry

        lax.fori_loop(0, steps, columns_of, 0)

    def pass_on(kind, h, j):
        index = 2 * kind + h
        return send(
            pre_out.at[kind, h],
            pre_in.at[kind, h],
            pre_send.at[index],
            pre_recv.at[index],
            in_sect(j),
        )

    pre_copies = {}
    for kind in range(2):
        for h in range(2):

            def store_out(which, target, product):
                pre_out[kind, h, which, :, target] = product.astype(bf16)

            products(3 if kind == 0 else first[h], h, store_out)
            pre_copies[kind, h] = pass_on(kind, h, first[h])
    for h in range(2):

        def store_pass(which, target, product):
            pre_own[h, which, :, target] = product

        products(second[h], h, store_pass)
    for h in range(2):
        pre_copies[0, h].wait_recv()

        def add_pass(n, carry):
            target = pl.ds(pl.multiple_of(n * TILE, TILE), TILE)
            for which in range(2):
                total = pre_own[h, which, :, target] + pre_in[0, h, which, :, target].astype(f32)
                pre_out[2, h, which, :, target] = total.astype(bf16)
            return carry

        lax.fori_loop(0, steps, add_pass, 0)
        pre_copies[2, h] = pass_on(2, h, second[h])
    for h in range(2):

        def store_own(which, target, product):
            pre_own[h, which, :, target] = product

        products(0, h, store_own)

    for copy in square_copies:
        copy.wait_recv()
    summed = square_out[:, 0:1]
    for j in range(1, n_sect):
        summed = summed + square_in[j, :, 0:1]
    features = n_sect * n_tp * width
    scale = lax.rsqrt(summed / features + norm_epsilon)
    act_copies = {}

    def share_act(j, h, block, to):
        index = 2 * j + h
        act_copies[j, h] = send(
            act_all.at[block, h],
            act_all.at[block, h],
            act_send.at[index],
            act_recv.at[index],
            in_sect(to),
        )

    for h in range(2):
        pre_copies[1, h].wait_recv()
        pre_copies[2, h].wait_recv()

        def activate(n, carry):
            target = pl.ds(pl.multiple_of(n * TILE, TILE), TILE)
            sums = []
            for which in range(2):
                total = pre_own[h, which, :, target] + pre_in[1, h, which, :, target].astype(f32)
                total = total + pre_in[2, h, which, :, target].astype(f32)
                sums.append(total * scale)
            active = sums[0] / (1.0 + jnp.exp(-sums[0])) * sums[1]
            act_all[sect, h, :, target] = active.astype(bf16)
            return carry

        lax.fori_loop(0, steps, activate, 0)
        share_act(first[h], h, sect, first[h])
    for h in range(2):
        share_act(second[h], h, sect, second[h])

    loaded(3)
    order = ((0, 0), (0, 1), (1, 0), (2, 1), (1, 1), (2, 0), (3, 0), (3, 1))
    rounds = [(unit, (0, 1)) for unit in order[:-2]]
    rounds += [(unit, (side,)) for side in range(2) for unit in order[-2:]]
    for place, ((j, h), sides) in enumerate(rounds):
        partner = flip(sect, j)
        if j and sides != (1,):
            act_copies[j, h].wait_recv()
        if (j, h) in ((1, 0), (2, 1)):
            share_act(3, h, partner, second[h])
        last = (j, h) == order[-1]
        depth = pl.ds(pl.multiple_of(partner * share + h * part_width, part_width), part_width)
        for side in sides:
            owner = pair if side == 0 else tp

            def down_columns(n, carry):
                source = pl.ds(pl.multiple_of(owner * width + n * TILE, TILE), TILE)
                target = pl.ds(pl.multiple_of(n * TILE, TILE), TILE)
                product = jnp.dot(
                    act_all[partner, h], down_w[depth, source], preferred_element_type=f32
                )
                if place:
                    product = product + down_own[side, :, target]
                if last and side == 0:
                    pair_out[:, target] = product.astype(bf16)
                else:
                    down_own[side, :, target] = product
                return carry

            lax.fori_loop(0, width // TILE, down_columns, 0)
            if last and side == 0:
                pair_copy = send(pair_out, pair_in, pair_send, pair_recv, in_pair)
    pair_copy.wait_recv()
    expert_out[...] = (
        (down_own[1] + pair_in[...].astype(f32)).astype(bf16).reshape(n_dp, cap, width)
    )
    back_copies = [
        send(
            expert_out.at[flip(dp, i)],
            returned.at[dp],
            back_send.at[i],
            back_recv.at[i],
            in_line(i),
        )
        for i in range(n_dp - 1, 0, -1)
    ]
    returned[dp] = expert_out[dp]

    for copy in stat_copies:
        copy.wait_recv()
    stats = stat_in[0]
    for j in range(1, group):
        stats = stats + stat_in[j]
    token_scale = lax.rsqrt(stats[1, 0:1, 0:tokens] / features + norm_epsilon)
    logits = stats[0, :, 0:tokens] * token_scale
    chosen = [jnp.sum(logits * onehot[k], axis=0, keepdims=True) for k in range(2)]
    weights = jnp.zeros((slots, tokens), f32)
    for k in range(2):
        mixing = 1.0 / (1.0 + jnp.exp(chosen[1 - k] - chosen[k]))
        weights = weights + hit[k] * mixing
    high = weights.astype(bf16)
    low = (weights - high.astype(f32)).astype(bf16)
    for copy in back_copies:
        copy.wait_recv()
    back = returned[...].reshape(slots, width)
    tn = (((0,), (0,)), ((), ()))
    combined = lax.dot_general(high, back, tn, preferred_element_type=f32) + lax.dot_general(
        low, back, tn, preferred_element_type=f32
    )
    out_ref[...] = (hidden[...].astype(f32) + combined).astype(out_ref.dtype)

    for copies in (att_copies, row_copies, pre_copies, act_copies):
        for copy in copies.values():
            copy.wait_send()
    for copy in stat_copies + square_copies + back_copies + [pair_copy]:
        copy.wait_send()


def fused_layer(
    queries,
    key_cache,
    cached_values,
    incoming_keys,
    incoming_values,
    lengths,
    residual,
    out_proj,
    norm_gain,
    router,
    gate_proj,
    up_proj,
    down_proj,
    routes,
):
    n_sect, n_dp, n_tp = (lax.axis_size(name) for name in ("sect", "dp", "tp"))
    group = n_sect * n_tp
    tokens, width = residual.shape
    experts = router.shape[1]
    cap = tokens // 2
    slots = experts * cap
    rows = n_dp * cap
    share = gate_proj.shape[1] // n_sect
    f32, bf16 = jnp.float32, jnp.bfloat16
    vmem = pl.BlockSpec(memory_space=pltpu.VMEM)
    hbm = pl.BlockSpec(memory_space=pl.ANY)
    dma = pltpu.SemaphoreType.DMA
    seq, heads, head_size = queries.shape
    buffers = [
        (key_cache.shape, bf16),
        (cached_values.shape, bf16),
        (queries.shape, f32),
        ((heads, seq, head_size), bf16),
        (out_proj.shape, bf16),
        (gate_proj.shape, bf16),
        (up_proj.shape, bf16),
        (down_proj.shape, bf16),
        ((n_tp, heads, tokens, head_size), bf16),
        ((tokens, width), bf16),
        ((2, slots, tokens), f32),
        ((experts, cap, width), bf16),
        ((n_tp, rows, width), bf16),
        ((rows, n_tp * width), bf16),
        ((rows, 128), f32),
        ((n_sect, rows, 128), f32),
        ((3, 2, 2, rows, share // 2), bf16),
        ((3, 2, 2, rows, share // 2), bf16),
        ((2, 2, rows, share // 2), f32),
        ((n_sect, 2, rows, share // 2), bf16),
        ((2, rows, width), f32),
        ((rows, width), bf16),
        ((rows, width), bf16),
        ((n_dp, cap, width), bf16),
        ((experts, cap, width), bf16),
        ((2, 8, 128), f32),
        ((group, 2, 8, 128), f32),
    ]
    semaphores = [dma((2, 4)), dma((4,))]
    for count in (2 * n_sect, 2 * n_dp, group, n_sect, 6, 2 * n_sect):
        semaphores += [dma((count,)), dma((count,))]
    semaphores += [dma, dma, dma((n_dp,)), dma((n_dp,))]
    return pl.pallas_call(
        functools.partial(layer_kernel, (n_sect, n_dp, n_tp)),
        out_shape=jax.ShapeDtypeStruct((tokens, width), bf16),
        in_specs=[vmem] * 3
        + [pl.BlockSpec(memory_space=pltpu.SMEM)]
        + [vmem] * 4
        + [hbm] * 6,
        out_specs=vmem,
        scratch_shapes=[pltpu.VMEM(shape, kind) for shape, kind in buffers] + semaphores,
        compiler_params=pltpu.CompilerParams(
            collective_id=0, has_side_effects=True, vmem_limit_bytes=62 * 1024 * 1024
        ),
    )(
        queries,
        incoming_keys,
        incoming_values,
        lengths,
        residual,
        norm_gain.reshape(group, 1, width),
        router.T,
        routes.T,
        key_cache,
        cached_values,
        out_proj,
        gate_proj,
        up_proj,
        down_proj,
    )


def per_device(
    queries,
    key_cache,
    cached_values,
    incoming_keys,
    incoming_values,
    lengths,
    residual,
    out_proj,
    norm_gain,
    router,
    gate_proj,
    up_proj,
    down_proj,
    routes,
):
    fits = lax.axis_size("sect") == 4 and lax.axis_size("tp") == 2
    if fits and residual.shape[1] % TILE == 0:
        return fused_layer(
            queries[0],
            key_cache[0],
            cached_values[0],
            incoming_keys[0],
            incoming_values[0],
            lengths,
            residual,
            out_proj,
            norm_gain,
            router,
            gate_proj[0],
            up_proj[0],
            down_proj[0],
            routes,
        )
    attended = attend(
        queries[0], key_cache[0], cached_values[0], incoming_keys[0], incoming_values[0], lengths[0]
    )
    seq_local = attended.shape[0]
    tp_count = lax.axis_size("tp")
    head_width = attended.shape[1]
    column_count = out_proj.shape[1]
    weight_split = out_proj.reshape(tp_count, head_width, column_count)
    initial = jnp.zeros((residual.shape[0], column_count), jnp.float32)
    shards = lax.all_gather(attended[None], ("sect", "tp"), axis=0, tiled=True)

    def add_one(counter, current):
        head_block = lax.dynamic_index_in_dim(shards, counter, 0, keepdims=False)
        weight = lax.dynamic_index_in_dim(weight_split, counter % tp_count, 0, keepdims=False)
        product = jnp.dot(head_block, weight, preferred_element_type=jnp.float32)
        row_start = counter // tp_count * seq_local
        earlier = lax.dynamic_slice_in_dim(current, row_start, seq_local, 0)
        return lax.dynamic_update_slice_in_dim(current, earlier + product, row_start, 0)

    projected = lax.fori_loop(0, shards.shape[0], add_one, initial)
    hidden = (residual.astype(jnp.float32) + projected).astype(jnp.bfloat16)
    group_rows = residual.shape[0]
    capacity = group_rows // 2
    expert_count = router.shape[1]
    slot_total = expert_count * capacity
    flat_routes = routes.reshape(-1)
    onehot = (flat_routes[:, None] == jnp.arange(expert_count, dtype=jnp.int32)[None, :]).astype(
        jnp.int32
    )
    earlier_count = jnp.cumsum(onehot, axis=0) - onehot
    target = flat_routes * capacity + jnp.sum(earlier_count * onehot, axis=1)
    matches = target[None, :] == jnp.arange(slot_total, dtype=jnp.int32)[:, None]
    route_token = jnp.arange(flat_routes.shape[0], dtype=jnp.int32) // 2
    slot_token = jnp.sum(jnp.where(matches, route_token[None, :], 0), axis=1)
    slot_used = jnp.any(matches, axis=1)
    full_width = lax.all_gather(hidden, ("sect", "tp"), axis=1, tiled=True)
    normed = normalize(full_width, norm_gain)
    logits = jnp.dot(normed, router, preferred_element_type=jnp.float32)
    chosen = jnp.take_along_axis(logits, routes, axis=1)
    mixing = jax.nn.sigmoid(chosen - chosen[:, ::-1])
    own_share = width_share(normed)
    taken = jnp.take(own_share, slot_token, axis=0)
    outgoing = jnp.where(slot_used[:, None], taken, jnp.zeros((), own_share.dtype)).reshape(
        expert_count, 1, capacity, own_share.shape[1]
    )
    returned = lax.all_to_all(
        expert_ffn(
            lax.all_to_all(outgoing, "dp", split_axis=0, concat_axis=1, tiled=True),
            gate_proj,
            up_proj,
            down_proj,
        ),
        "dp",
        split_axis=1,
        concat_axis=0,
        tiled=True,
    )
    mix_flat = mixing.reshape(-1)
    returned_rows = returned.reshape(slot_total, -1)[target].astype(jnp.float32)
    combined = jnp.sum(
        mix_flat.reshape(group_rows, 2)[:, :, None] * returned_rows.reshape(group_rows, 2, -1),
        axis=1,
    )
    return (hidden.astype(jnp.float32) + combined).astype(jnp.bfloat16)


def solution(mesh):
    placed = (
        P("dp", "sect", "tp", None),
        P("dp", "sect", "tp", None, None),
        P("dp", "sect", "tp", None, None),
        P("dp", "sect", "tp", None),
        P("dp", "sect", "tp", None),
        P("dp", "sect"),
        P("dp", ("sect", "tp")),
        P(None, ("sect", "tp")),
        P(),
        P(),
        P("dp", "sect", "tp"),
        P("dp", "sect", "tp"),
        P("dp", "tp", "sect"),
        P("dp", None),
    )
    return jax.shard_map(
        per_device, mesh=mesh, in_specs=placed, out_specs=P("dp", ("sect", "tp")), check_vma=False
    )
```
